512 devices in a mesh: gx: 8 (over z_lo), gy: 8 (over y, z_hi), gz: 8 (over x, core).
Axes of the slice: x: 4, y: 4, z: 16 (z_hi: 2, z_lo: 8; z = z_hi * 8 + z_lo), core: 2. Of those that a mesh axis runs over, the one named last changes fastest.
Arguments:
- mid_stream: bfloat16 [1024, 7168], P('gz', ('gx', 'gy')), may hold values from -6 to 6
- out_grad: bfloat16 [1024, 7168], P('gz', ('gx', 'gy')), may hold values from -6 to 6
- attn_values: bfloat16 [1024, 7168], P(('gz', 'gx'), 'gy'), may hold values from -6 to 6
- attn_gate: bfloat16 [7168], P(('gx', 'gy')), may hold values from 0.099609375 to 1.8984375
- ffn_gate: bfloat16 [7168], P(('gx', 'gy')), may hold values from 0.099609375 to 1.8984375
- up_weight: bfloat16 [14336, 7168], P(('gy', 'gz'), 'gx'), may hold values from -0.0625 to 0.0625
- down_weight: bfloat16 [14336, 7168], P(('gy', 'gz'), 'gx'), may hold values from -0.046875 to 0.046875
- proj_weight: bfloat16 [7168, 7168], P(('gx', 'gz'), 'gy'), may hold values from -0.0625 to 0.0625
Outputs:
- grad_mid: bfloat16 [1024, 7168], P('gz', ('gx', 'gy'))
- grad_attn: bfloat16 [1024, 7168], P(('gz', 'gx'), 'gy')
- grad_proj: bfloat16 [7168, 7168], P(('gx', 'gz'), 'gy')
- grad_up: bfloat16 [14336, 7168], P(('gy', 'gz'), 'gx')
- grad_down: bfloat16 [14336, 7168], P(('gy', 'gz'), 'gx')
The draws below stay inside these ranges and needn't reach their ends.
All inputs are finite; a program needn't handle non-finite values.
Results may differ from the reference program's by a relative error of at most 0.025.
Values may be sent and summed in bfloat16 or wider, within the bound.
A program may use at most 64 MiB of HBM per device.

```python
import jax
import jax.numpy as jnp
from jax import lax

D = 7168
FF = 14336
TOKENS = 1024
N_GX = 8


def levels(key, extent, pieces, smallest, high):
    gain, own = 1.0, jax.random.fold_in(key, 6)
    for dim, blocks in pieces:
        heights = jnp.exp(jax.random.uniform(jax.random.fold_in(own, dim), (blocks,), jnp.float32, smallest / len(pieces), high / len(pieces)))
        gain = gain * jnp.repeat(heights, extent[dim] // blocks).reshape([-1 if axis == dim else 1 for axis in range(len(extent))])
    return gain


def centred(own_key, shape, spread, bound, pieces=(), held_as=jnp.bfloat16):
    level = levels(own_key, shape, pieces, -0.22, 0.18) if pieces else 1.0
    result = jax.random.normal(own_key, shape, jnp.float32) * spread * level
    return jnp.minimum(jnp.maximum(result, -bound), bound).astype(held_as)


def setup_inputs(seed: int = 0) -> dict:
    arg_keys = jax.random.split(jax.random.key(seed), 9)
    mid_stream = centred(arg_keys[0], (TOKENS, D), 1.0, 6.0, ((0, 8), (1, 64)))
    out_grad = centred(arg_keys[1], (TOKENS, D), 1.0, 6.0, ((0, 8), (1, 64)))
    attn_values = centred(arg_keys[2], (TOKENS, D), 1.0, 6.0, ((0, 64), (1, 8)))
    attn_gate = jnp.clip(1.0 + 0.18 * jax.random.normal(arg_keys[3], (D,), jnp.float32), 0.099609375, 1.8984375).astype(jnp.bfloat16)
    ffn_gate = jnp.clip(1.0 + 0.18 * jax.random.normal(arg_keys[4], (D,), jnp.float32), 0.099609375, 1.8984375).astype(jnp.bfloat16)
    up_weight = centred(arg_keys[5], (FF, D), D ** -0.5, 0.0625, ((0, 64), (1, 8)))
    down_weight = centred(arg_keys[6], (FF, D), FF ** -0.5, 0.046875, ((0, 64), (1, 8)))
    proj_weight = centred(arg_keys[7], (D, D), D ** -0.5, 0.0625, ((0, 64), (1, 8)))
    return dict(mid_stream=mid_stream, out_grad=out_grad, attn_values=attn_values, attn_gate=attn_gate, ffn_gate=ffn_gate, up_weight=up_weight, down_weight=down_weight, proj_weight=proj_weight)


root_two_pi = 0.7978845608028654
cubic_term = 0.044715


def gelu_value(values):
    inside = root_two_pi * (values + cubic_term * values * values * values)
    return 0.5 * values * (1.0 + jnp.tanh(inside))


def gelu_slope(values):
    tangent = jnp.tanh(root_two_pi * (values + cubic_term * values * values * values))
    return 0.5 * (1.0 + tangent) + 0.5 * values * (1.0 - tangent * tangent) * root_two_pi * (1.0 + 3.0 * cubic_term * values * values)


def reference(mid_stream, out_grad, attn_values, attn_gate, ffn_gate, up_weight, down_weight, proj_weight):
    factor = float(TOKENS) ** -0.5
    span = D // N_GX
    gated_grad = (out_grad.astype(jnp.float32) * ffn_gate.astype(jnp.float32)).astype(jnp.bfloat16)
    pre_gelu = jnp.zeros((TOKENS, FF), jnp.float32)
    gelu_grad = jnp.zeros((TOKENS, FF), jnp.float32)
    for index in range(N_GX):
        lower = index * span
        upper = lower + span
        up_term = jnp.dot(mid_stream[:, lower:upper], up_weight[:, lower:upper].T, preferred_element_type=jnp.float32)
        pre_gelu = pre_gelu + lax.optimization_barrier(up_term.astype(jnp.bfloat16)).astype(jnp.float32)
        down_term = jnp.dot(gated_grad[:, lower:upper], down_weight[:, lower:upper].T, preferred_element_type=jnp.float32)
        gelu_grad = gelu_grad + lax.optimization_barrier(down_term.astype(jnp.bfloat16)).astype(jnp.float32)
    hidden = gelu_value(pre_gelu).astype(jnp.bfloat16)
    hidden_grad = (gelu_grad * gelu_slope(pre_gelu)).astype(jnp.bfloat16)
    grad_down = (jnp.dot(hidden.T, gated_grad, preferred_element_type=jnp.float32) * factor).astype(jnp.bfloat16)
    grad_up = (jnp.dot(hidden_grad.T, mid_stream, preferred_element_type=jnp.float32) * factor).astype(jnp.bfloat16)
    mid_total = out_grad.astype(jnp.float32) + jnp.dot(hidden_grad, up_weight, preferred_element_type=jnp.float32)
    grad_mid = mid_total.astype(jnp.bfloat16)
    gated_mid = (mid_total * attn_gate.astype(jnp.float32)).astype(jnp.bfloat16)
    grad_proj = (jnp.dot(gated_mid.T, attn_values, preferred_element_type=jnp.float32) * factor).astype(jnp.bfloat16)
    grad_attn = jnp.dot(gated_mid, proj_weight, preferred_element_type=jnp.float32).astype(jnp.bfloat16)
    return (grad_mid, grad_attn, grad_proj, grad_up, grad_down)
```

```python
import functools

import jax
import jax.numpy as jnp
from jax import lax
from jax.experimental import pallas as pl
from jax.experimental.pallas import tpu as pltpu
from jax.sharding import PartitionSpec as P

MESH = pl.DeviceIdType.MESH
BF16, F32 = jnp.bfloat16, jnp.float32
root_two_pi = 0.7978845608028654
cubic_term = 0.044715


def dot(former, latter, contract):
    return lax.dot_general(
        former, latter, ((contract[:1], contract[1:]), ((), ())), preferred_element_type=F32
    )


def gelu_pair(values):
    square = values * values
    tangent = jnp.tanh(root_two_pi * (values + cubic_term * values * square))
    half = 0.5 * (1.0 + tangent)
    slope = half + 0.5 * values * (1.0 - tangent * tangent) * root_two_pi * (
        1.0 + 3.0 * cubic_term * square
    )
    return values * half, slope


def kernel(
    factor,
    mid_ref, out_ref, attn_ref, agate_ref, fgate_ref, up_ref, down_ref, proj_ref,
    gmid_ref, gattn_ref, gproj_ref, gup_ref, gdown_ref,
    G, part, from_outer, from_mid, H, up_all, proj_all, attn_all, gates, og_t,
    HG, back, tot, back_send, yr, t_send, hr, GM, GP, ap, ar, acc,
    rs_s, rs_r, xm_s, xm_r, ag_s, ag_r, dp_s, dp_r, send_sems, recv_sems,
):
    feats, toks = mid_ref.shape[1], mid_ref.shape[0]
    units = up_ref.shape[0]
    a = lax.axis_index("gx")
    gy = lax.axis_index("gy")
    gz = lax.axis_index("gz")
    x, c = gz // 2, lax.rem(gz, 2)
    y, h = gy // 2, lax.rem(gy, 2)

    def xpeer(d):
        return {"gz": lax.rem(x + d, 4) * 2 + c}

    def ypeer(d):
        return {"gy": lax.rem(y + d, 4) * 2 + h}

    core = {"gz": x * 2 + 1 - c}
    hpeer = {"gy": y * 2 + 1 - h}

    def gxpeer(d):
        return {"gx": lax.rem(a + d, 8)}

    def gzpeer(d):
        return {"gz": lax.rem(gz + d, 8)}

    barrier = pltpu.get_barrier_semaphore()
    peers = [gzpeer(d) for d in range(1, 8)] + [gxpeer(d) for d in range(1, 8)]
    peers += [ypeer(d) for d in range(1, 4)] + [hpeer]
    for peer in peers:
        pl.semaphore_signal(barrier, inc=1, device_id=peer, device_id_type=MESH)

    sent = []
    count = [0]

    def put(src, dst, peer):
        index = count[0]
        count[0] += 1
        copy = pltpu.make_async_remote_copy(
            src, dst, send_sems.at[index], recv_sems.at[index],
            device_id=peer, device_id_type=MESH,
        )
        copy.start()
        sent.append(copy)
        return copy

    lanes = pl.ds(pl.multiple_of(c * toks, toks), toks)
    other_lanes = pl.ds(pl.multiple_of((1 - c) * toks, toks), toks)
    own_rows = pl.ds(pl.multiple_of(gy * feats, 16), feats)
    y_rows = pl.ds(pl.multiple_of(y * 2 * feats, 32), 2 * feats)
    h_rows = pl.ds(pl.multiple_of(h * feats, 16), feats)

    out_grad = out_ref[...].astype(F32)
    gated = (out_grad * fgate_ref[...].astype(F32)).astype(BF16).astype(F32)
    G[x, 0, own_rows, lanes] = mid_ref[...].astype(F32).T.astype(BF16)
    G[x, 1, own_rows, lanes] = gated.T.astype(BF16)
    og_t[...] = out_grad.T
    gates[h_rows, :] = jnp.broadcast_to(agate_ref[...].astype(F32), (toks, feats)).T.astype(BF16)

    pl.semaphore_wait(barrier, len(peers))

    h_copy = put(G.at[x, :, own_rows, lanes], G.at[x, :, own_rows, lanes], hpeer)
    gate_copy = put(gates.at[h_rows, :], gates.at[h_rows, :], hpeer)
    attn_row = pl.ds(pl.multiple_of((gz * 8 + a) * 16, 16), 16)
    attn_all[attn_row, :] = attn_ref[...]
    up_all[gz] = up_ref[...]
    proj_all[gz] = proj_ref[...]
    h_copy.wait_recv()
    mid_y = [put(G.at[x, 0, y_rows, lanes], G.at[x, 0, y_rows, lanes], ypeer(d)) for d in (1, 3, 2)]
    gat_x = [put(G.at[x, 1, y_rows, lanes], G.at[x, 1, y_rows, lanes], xpeer(d)) for d in (1, 3, 2)]
    attn_z = [put(attn_ref, attn_all.at[attn_row, :], gxpeer(d)) for d in range(1, 8)]
    for copy in mid_y:
        copy.wait_recv()
    mid_x = [put(G.at[x, 0, :, lanes], G.at[x, 0, :, lanes], xpeer(d)) for d in (1, 3, 2)]
    mid_c = [put(G.at[x, 0, :, lanes], G.at[x, 0, :, lanes], core)]
    for copy in gat_x:
        copy.wait_recv()
    gat_y = [put(G.at[:, 1, y_rows, lanes], G.at[:, 1, y_rows, lanes], ypeer(d)) for d in (1, 3, 2)]
    for copy, d in zip(mid_x, (1, 3, 2)):
        copy.wait_recv()
        block = lax.rem(x - d + 4, 4)
        mid_c.append(put(G.at[block, 0, :, lanes], G.at[block, 0, :, lanes], core))
    for copy in gat_y:
        copy.wait_recv()
    gat_c = put(G.at[:, 1, :, lanes], G.at[:, 1, :, lanes], core)

    up_x = [put(up_ref, up_all.at[gz], xpeer(d)) for d in (1, 3, 2)]
    proj_x = [put(proj_ref, proj_all.at[gz], xpeer(d)) for d in (1, 3, 2)]
    up_c = [put(up_ref, up_all.at[gz], core)]
    proj_c = [put(proj_ref, proj_all.at[gz], core)]
    for copy in attn_z:
        copy.wait_recv()

    def attn_rows(block):
        return pl.ds(pl.multiple_of(block * toks, toks), toks)

    own = attn_all.at[attn_rows(gz), :]
    attn_x = [put(own, own, xpeer(d)) for d in (1, 3, 2)]
    attn_c = [put(own, own, core)]

    for copy in mid_c:
        copy.wait_recv()
    gat_c.wait_recv()

    near = a < 4
    place = jnp.where(near, a, 7 - a)
    inner = {"gx": jnp.where(near, a + 1, a - 1)}
    outer = {"gx": jnp.clip(jnp.where(near, a - 1, a + 1), 0, 7)}
    lag = 4 - place

    def rs_copy(m):
        return pltpu.make_async_remote_copy(
            part.at[m], from_outer.at[m], rs_s.at[m], rs_r.at[m],
            device_id=inner, device_id_type=MESH)

    def xm_copy(m):
        return pltpu.make_async_remote_copy(
            part.at[m], from_mid.at[m], xm_s.at[m], xm_r.at[m],
            device_id=inner, device_id_type=MESH)

    def ag_copy(t, s):
        return pltpu.make_async_remote_copy(
            H.at[t, s], H.at[t, s], ag_s.at[t, s], ag_r.at[t, s],
            device_id=outer, device_id_type=MESH)

    def dp_same(k):
        t = lax.rem(x + k, 4)
        return pltpu.make_async_remote_copy(
            H.at[t, 1, :, lanes], HG.at[gz], dp_s.at[k, 0], dp_r.at[k, 0],
            device_id={"gz": t * 2 + c}, device_id_type=MESH)

    def dp_other(k):
        t = lax.rem(x + k, 4)
        return pltpu.make_async_remote_copy(
            H.at[t, 1, :, other_lanes], HG.at[gz], dp_s.at[k, 1], dp_r.at[k, 1],
            device_id={"gz": t * 2 + 1 - c}, device_id_type=MESH)

    def line_step(i, carry):
        @pl.when(i < 4)
        def _():
            t = lax.rem(x + i, 4)
            for s in range(2):
                m = i * 2 + s
                weight = up_ref if s == 0 else down_ref
                term = dot(weight[...], G[t, s], (1, 0))

                @pl.when(place == 0)
                def _():
                    part[m] = term.astype(BF16)

                @pl.when(place > 0)
                def _():
                    rs_copy(m).wait_recv()
                    part[m] = (term + from_outer[m].astype(F32)).astype(BF16)

                @pl.when(place < 3)
                def _():
                    rs_copy(m).start()

                @pl.when(place == 3)
                def _():
                    xm_copy(m).start()

        k = i - lag

        @pl.when((k >= 0) & (k < 4))
        def _():
            t = lax.rem(x + k, 4)

            @pl.when(place == 3)
            def _():
                xm_copy(2 * k).wait_recv()
                xm_copy(2 * k + 1).wait_recv()

                def rows_step(r, carry):
                    rows = pl.ds(pl.multiple_of(r * 32, 32), 32)
                    pre = part[2 * k, rows, :].astype(F32) + from_mid[2 * k, rows, :].astype(F32)
                    grad = part[2 * k + 1, rows, :].astype(F32) + from_mid[2 * k + 1, rows, :].astype(F32)
                    value, slope = gelu_pair(pre)
                    H[t, 0, rows, :] = value.astype(BF16)
                    H[t, 1, rows, :] = (grad * slope).astype(BF16)
                    return carry

                lax.fori_loop(0, units // 32, rows_step, 0)
                ag_copy(t, 1).start()
                ag_copy(t, 0).start()

            @pl.when(place < 3)
            def _():
                ag_copy(t, 1).wait_recv()

                @pl.when(place > 0)
                def _():
                    ag_copy(t, 1).start()

            @pl.when(k == 0)
            def _():
                HG[gz] = H[t, 1, :, lanes]

            @pl.when(k > 0)
            def _():
                dp_same(k).start()

            dp_other(k).start()

            @pl.when(place < 3)
            def _():
                ag_copy(t, 0).wait_recv()

                @pl.when(place > 0)
                def _():
                    ag_copy(t, 0).start()

        return carry

    lax.fori_loop(0, 8, line_step, 0)

    def hand_over(copies, ref_of, held):
        for copy, d in zip(copies, (1, 3, 2)):
            copy.wait_recv()
            block = lax.rem(x - d + 4, 4) * 2 + c
            held.append(put(ref_of(block), ref_of(block), core))

    hand_over(up_x, lambda block: up_all.at[block], up_c)
    hand_over(proj_x, lambda block: proj_all.at[block], proj_c)
    hand_over(attn_x, lambda block: attn_all.at[attn_rows(block), :], attn_c)

    for k in range(4):
        if k:
            dp_same(k).wait_recv()
        dp_other(k).wait_recv()
    for copy in up_c:
        copy.wait_recv()

    back[...] = dot(HG[0], up_all[0], (0, 0))

    def back_step(g, carry):
        back[...] += dot(HG[g], up_all[g], (0, 0))
        return carry

    lax.fori_loop(1, 8, back_step, 0)
    total_t = back[...].T
    back_send[...] = total_t.astype(BF16)
    y_rows_of = lambda d: pl.ds(pl.multiple_of(lax.rem(y + d, 4) * 2 * feats, 32), 2 * feats)
    y_sum = [put(back_send.at[y_rows_of(d), :], yr.at[d - 1], ypeer(d)) for d in (1, 3, 2)]

    def grad_weight(s, g, out):
        acc[...] = dot(H[0, s], G[0, g], (1, 1))

        def step(t, carry):
            acc[...] += dot(H[t, s], G[t, g], (1, 1))
            return carry

        lax.fori_loop(1, 4, step, 0)
        out[...] = (acc[...] * factor).astype(BF16)

    grad_weight(1, 0, gup_ref)
    for copy in y_sum:
        copy.wait_recv()
    total = back_send[y_rows, :].astype(F32)
    for d in range(3):
        total = total + yr[d].astype(F32)
    tot[...] = total
    tot[h_rows, :] += og_t[...]
    t_send[...] = tot[...].astype(BF16)
    h_sum = put(t_send, hr, hpeer)
    grad_weight(0, 1, gdown_ref)
    gate_copy.wait_recv()
    h_sum.wait_recv()
    total = tot[...] + hr[...].astype(F32)
    GM[y_rows, :] = (total * gates[...].astype(F32)).astype(BF16)
    gm_y = [put(GM.at[y_rows, :], GM.at[y_rows, :], ypeer(d)) for d in (1, 3, 2)]
    tot[...] = total
    gmid_ref[...] = tot[h_rows, :].T.astype(BF16)
    for copy in proj_c:
        copy.wait_recv()
    for copy in gm_y:
        copy.wait_recv()

    gp_copies = []
    feat_rows = lambda g: pl.ds(pl.multiple_of(g * feats, 16), feats)
    gz_lanes = pl.ds(pl.multiple_of(gz * toks, toks), toks)
    for d in range(1, 8):
        target = lax.rem(gz + d, 8)
        gp_copies.append(put(GM.at[feat_rows(target), :], GP.at[:, gz_lanes], gzpeer(d)))
    GP[:, gz_lanes] = GM[feat_rows(gz), :]
    back[...] = dot(GM[feat_rows(0), :], proj_all[0], (0, 0))

    def proj_step(g, carry):
        back[...] += dot(GM[feat_rows(g), :], proj_all[g], (0, 0))
        return carry

    lax.fori_loop(1, 8, proj_step, 0)
    ap[...] = back[...].astype(BF16).reshape(ap.shape)
    ar_copies = [put(ap.at[lax.rem(a + d, 8)], ar.at[d - 1], gxpeer(d)) for d in (4, 3, 5, 2, 6, 1, 7)]
    for copy in attn_c:
        copy.wait_recv()
    for copy in gp_copies:
        copy.wait_recv()
    gproj_ref[...] = (dot(GP[...], attn_all[...], (1, 0)) * factor).astype(BF16)
    for copy in ar_copies:
        copy.wait_recv()
    total = ap[a].astype(F32)
    for d in range(7):
        total = total + ar[d].astype(F32)
    gattn_ref[...] = total.astype(BF16)

    for copy in sent:
        copy.wait_send()

    def drain(m, carry):
        @pl.when(place < 3)
        def _():
            rs_copy(m).wait_send()

        @pl.when(place == 3)
        def _():
            xm_copy(m).wait_send()

        @pl.when(place > 0)
        def _():
            ag_copy(m // 2, lax.rem(m, 2)).wait_send()

        return carry

    lax.fori_loop(0, 8, drain, 0)
    for k in range(4):
        if k:
            dp_same(k).wait_send()
        dp_other(k).wait_send()


def per_device(
    mid_stream, out_grad, attn_values, attn_gate, ffn_gate, up_weight, down_weight, proj_weight
):
    toks, feats = mid_stream.shape
    units, wide = up_weight.shape
    tok_total = toks * lax.axis_size("gz")
    factor = float(tok_total) ** (-0.5)
    vmem = pl.BlockSpec(memory_space=pltpu.VMEM)
    pair = 2 * toks
    dma = pltpu.SemaphoreType.DMA
    scratch = [
        pltpu.VMEM((4, 2, wide, pair), BF16),
        pltpu.VMEM((8, units, pair), BF16),
        pltpu.VMEM((8, units, pair), BF16),
        pltpu.VMEM((8, units, pair), BF16),
        pltpu.VMEM((4, 2, units, pair), BF16),
        pltpu.VMEM((8, units, wide), BF16),
        pltpu.VMEM((8, feats, wide), BF16),
        pltpu.VMEM((tok_total, wide), BF16),
        pltpu.VMEM((2 * feats, toks), BF16),
        pltpu.VMEM((feats, toks), F32),
        pltpu.VMEM((8, units, toks), BF16),
        pltpu.VMEM((toks, wide), F32),
        pltpu.VMEM((2 * feats, toks), F32),
        pltpu.VMEM((wide, toks), BF16),
        pltpu.VMEM((3, 2 * feats, toks), BF16),
        pltpu.VMEM((2 * feats, toks), BF16),
        pltpu.VMEM((2 * feats, toks), BF16),
        pltpu.VMEM((wide, toks), BF16),
        pltpu.VMEM((feats, tok_total), BF16),
        pltpu.VMEM((8, toks // 8, wide), BF16),
        pltpu.VMEM((7, toks // 8, wide), BF16),
        pltpu.VMEM((units, wide), F32),
        dma((8,)), dma((8,)), dma((8,)), dma((8,)), dma((4, 2)), dma((4, 2)),
        dma((4, 2)), dma((4, 2)), dma((72,)), dma((72,)),
    ]
    shape = jax.ShapeDtypeStruct
    return pl.pallas_call(
        functools.partial(kernel, factor),
        out_shape=(
            shape((toks, feats), BF16),
            shape((attn_values.shape[0], wide), BF16),
            shape((feats, wide), BF16),
            shape((units, wide), BF16),
            shape((units, wide), BF16),
        ),
        in_specs=[vmem] * 8,
        out_specs=(vmem,) * 5,
        scratch_shapes=scratch,
        compiler_params=pltpu.CompilerParams(
            collective_id=0, has_side_effects=True, vmem_limit_bytes=48 * 1024 * 1024
        ),
        cost_estimate=pl.CostEstimate(flops=2_500_000_000, bytes_accessed=3_000_000, transcendentals=0),
        name="block_backward",
    )(
        mid_stream, out_grad, attn_values, attn_gate.reshape(1, feats), ffn_gate.reshape(1, feats),
        up_weight, down_weight, proj_weight,
    )


def solution(mesh):
    return jax.shard_map(
        per_device,
        mesh=mesh,
        in_specs=(
            P("gz", ("gx", "gy")),
            P("gz", ("gx", "gy")),
            P(("gz", "gx"), "gy"),
            P(("gx", "gy")),
            P(("gx", "gy")),
            P(("gy", "gz"), "gx"),
            P(("gy", "gz"), "gx"),
            P(("gx", "gz"), "gy"),
        ),
        out_specs=(
            P("gz", ("gx", "gy")),
            P(("gz", "gx"), "gy"),
            P(("gx", "gz"), "gy"),
            P(("gy", "gz"), "gx"),
            P(("gy", "gz"), "gx"),
        ),
        check_vma=False,
    )
```

```python
import functools

import jax
import jax.numpy as jnp
from jax import lax
from jax.experimental import pallas as pl
from jax.experimental.pallas import tpu as pltpu
from jax.sharding import PartitionSpec as P

MESH = pl.DeviceIdType.MESH
BF16, F32 = jnp.bfloat16, jnp.float32
root_two_pi = 0.7978845608028654
cubic_term = 0.044715


def dot(former, latter, contract):
    return lax.dot_general(
        former, latter, ((contract[:1], contract[1:]), ((), ())), preferred_element_type=F32
    )


def gelu_pair(values):
    square = values * values
    tangent = jnp.tanh(root_two_pi * (values + cubic_term * values * square))
    half = 0.5 * (1.0 + tangent)
    slope = half + 0.5 * values * (1.0 - tangent * tangent) * root_two_pi * (
        1.0 + 3.0 * cubic_term * square
    )
    return values * half, slope


def kernel(
    factor,
    mid_in, out_in, attn_in, agate_in, fgate_in, up_in, down_in, proj_in,
    gmid_ref, gattn_ref, gproj_ref, gup_ref, gdown_ref,
    G, term, part, from_outer, from_mid, H, up_all, down_own, proj_all, attn_all, gates, og, ag_row, fg_row,
    HG, back, tot, back_send, yr, t_send, hr, GM, GP, ap, ar, acc,
    rs_s, rs_r, xm_s, xm_r, ag_s, ag_r, dp_s, dp_r, send_sems, recv_sems, local_sems,
):
    feats, toks = mid_in.shape
    units = up_in.shape[0]
    units_order = ((0, 0), (1, 0), (1, 1), (2, 0), (2, 1), (3, 0), (3, 1), (0, 1))
    steps = len(units_order)
    lags = (steps, 6, 4, 1)
    a = lax.axis_index("gx")
    gy = lax.axis_index("gy")
    gz = lax.axis_index("gz")
    x, c = gz // 2, lax.rem(gz, 2)
    y, h = gy // 2, lax.rem(gy, 2)

    def xpeer(d):
        return {"gz": lax.rem(x + d, 4) * 2 + c}

    def ypeer(d):
        return {"gy": lax.rem(y + d, 4) * 2 + h}

    core = {"gz": x * 2 + 1 - c}
    hpeer = {"gy": y * 2 + 1 - h}

    def gxpeer(d):
        return {"gx": lax.rem(a + d, 8)}

    def gzpeer(d):
        return {"gz": lax.rem(gz + d, 8)}

    barrier = pltpu.get_barrier_semaphore()
    peers = [gzpeer(d) for d in range(1, 8)] + [gxpeer(d) for d in range(1, 8)]
    peers += [ypeer(d) for d in range(1, 4)] + [hpeer]
    for peer in peers:
        pl.semaphore_signal(barrier, inc=1, device_id=peer, device_id_type=MESH)

    sent, open_recv = [], []
    count = [0]

    def put(src, dst, peer):
        index = count[0]
        count[0] += 1
        copy = pltpu.make_async_remote_copy(
            src, dst, send_sems.at[index], recv_sems.at[index],
            device_id=peer, device_id_type=MESH,
        )
        copy.start()
        sent.append(copy)
        open_recv.append(copy)
        return copy

    def arrive(copy):
        copy.wait_recv()
        open_recv[:] = [other for other in open_recv if other is not copy]

    def finish(line):
        for copy in open_recv:
            copy.wait_recv()
        for copy in sent:
            copy.wait_send()
        if not line:
            return

        for u in range(steps):
            for s in range(2):
                @pl.when(place < 3)
                def _():
                    rs_copy(s, u).wait_send()

                @pl.when(place == 3)
                def _():
                    xm_copy(s, u).wait_send()

                @pl.when(place > 0)
                def _():
                    ag_copy(s, u).wait_send()

        drain_spread(lambda copy: copy.wait_send())

    own_rows = pl.ds(pl.multiple_of(gy * feats, 16), feats)
    y_rows = pl.ds(pl.multiple_of(y * 2 * feats, 32), 2 * feats)
    h_rows = pl.ds(pl.multiple_of(h * feats, 16), feats)

    partner_rows = pl.ds(pl.multiple_of((y * 2 + 1 - h) * feats, 16), feats)
    attn_row = pl.ds(pl.multiple_of((gz * 8 + a) * 16, 16), 16)

    loads = [
        pltpu.make_async_copy(src, dst, local_sems.at[n])
        for n, (src, dst) in enumerate((
            (mid_in, G.at[x, c, 0, own_rows, :]),
            (out_in, og),
            (fgate_in, fg_row),
            (agate_in, ag_row),
            (up_in, up_all.at[gz]),
            (down_in, down_own),
            (proj_in, proj_all.at[gz]),
            (attn_in, attn_all.at[attn_row, :]),
        ))
    ]
    for load in loads:
        load.start()
    for load in loads[:4]:
        load.wait()

    def gate_columns(row):
        return jnp.broadcast_to(row[...].astype(F32), (toks, feats)).T

    G[x, c, 1, own_rows, :] = (og[...].astype(F32) * gate_columns(fg_row)).astype(BF16)
    gates[h_rows, :] = gate_columns(ag_row).astype(BF16)
    for load in loads[4:]:
        load.wait()

    pl.semaphore_wait(barrier, len(peers))

    near_first = (2, 1, 3)

    def block_from(d):
        return lax.rem(x - d + 4, 4)

    h_copy = put(G.at[x, c, :, own_rows, :], G.at[x, c, :, own_rows, :], hpeer)
    own_y = [put(G.at[x, c, :, own_rows, :], G.at[x, c, :, own_rows, :], ypeer(d)) for d in near_first]
    gat_x = [[put(G.at[x, c, 1, own_rows, :], G.at[x, c, 1, own_rows, :], xpeer(d))] for d in near_first]
    arrive(h_copy)
    own_y += [
        put(G.at[x, c, :, partner_rows, :], G.at[x, c, :, partner_rows, :], ypeer(d)) for d in near_first
    ]
    for copies, d in zip(gat_x, near_first):
        copies.append(put(G.at[x, c, 1, partner_rows, :], G.at[x, c, 1, partner_rows, :], xpeer(d)))
    own_attn = attn_all.at[attn_row, :]
    attn_z = [put(own_attn, own_attn, gxpeer(d)) for d in range(1, 8)]
    gate_copy = put(gates.at[h_rows, :], gates.at[h_rows, :], hpeer)
    for copy in own_y:
        arrive(copy)
    own_c = put(G.at[x, c], G.at[x, c], core)
    mid_x = [put(G.at[x, c, 0], G.at[x, c, 0], xpeer(d)) for d in near_first]
    gat_y = []
    for copies, d in zip(gat_x, near_first):
        for copy in copies:
            arrive(copy)
        rows = G.at[block_from(d), c, 1, y_rows, :]
        gat_y.append([put(rows, rows, ypeer(e)) for e in near_first])

    def acquire(n):
        block = block_from(near_first[n])
        arrive(mid_x[n])
        mid_rows, gat_rows = G.at[block, c, 0], G.at[block, c, 1]
        halves = [put(mid_rows, mid_rows, core)]
        for copy in gat_y[n]:
            arrive(copy)
        halves.append(put(gat_rows, gat_rows, core))
        for copy in halves:
            arrive(copy)

    def attn_rows(block):
        return pl.ds(pl.multiple_of(block * toks, toks), toks)

    def hand_over(copies, ref_of, held):
        for copy, d in zip(copies, near_first):
            arrive(copy)
            block = block_from(d) * 2 + c
            held.append(put(ref_of(block), ref_of(block), core))

    near = a < 4
    place = jnp.where(near, a, 7 - a)
    inner = {"gx": jnp.where(near, a + 1, a - 1)}
    outer = {"gx": jnp.clip(jnp.where(near, a - 1, a + 1), 0, 7)}
    def block_of(k):
        return lax.rem(x + (0, 2, 3, 1)[k], 4)

    def rs_copy(s, u):
        return pltpu.make_async_remote_copy(
            part.at[u, s], from_outer.at[u, s], rs_s.at[u, s], rs_r.at[u, s],
            device_id=inner, device_id_type=MESH)

    def xm_copy(s, u):
        return pltpu.make_async_remote_copy(
            part.at[u, s], from_mid.at[u, s], xm_s.at[u, s], xm_r.at[u, s],
            device_id=inner, device_id_type=MESH)

    def held_at(u, s):
        k, kind = units_order[u]
        return block_of(k), half_of(kind), s

    def half_of(kind):
        return 1 - c if kind else c

    def ag_copy(s, u):
        place_held = H.at[held_at(u, s)]
        return pltpu.make_async_remote_copy(
            place_held, place_held, ag_s.at[u, s], ag_r.at[u, s],
            device_id=outer, device_id_type=MESH)

    def dp_copy(k, kind):
        t, half = block_of(k), half_of(kind)
        return pltpu.make_async_remote_copy(
            H.at[t, half, 1], HG.at[gz], dp_s.at[k, kind], dp_r.at[k, kind],
            device_id={"gz": t * 2 + half}, device_id_type=MESH)

    def spread(u):
        k, kind = units_order[u]
        if k or kind:
            dp_copy(k, kind).start()
        else:
            HG[gz] = H[x, c, 1]

    def products(u):
        t, half, _ = held_at(u, 0)
        term[u % 2, 0] = dot(up_all[gz], G[t, half, 0], (1, 0))
        term[u % 2, 1] = dot(down_own[...], G[t, half, 1], (1, 0))

    def reduce_step(u):
        kind = u % 2
        for s in range(2):
            @pl.when(place == 0)
            def _():
                part[u, s] = term[kind, s].astype(BF16)

            @pl.when(place > 0)
            def _():
                rs_copy(s, u).wait_recv()
                part[u, s] = (term[kind, s] + from_outer[u, s].astype(F32)).astype(BF16)

            @pl.when(place < 3)
            def _():
                rs_copy(s, u).start()

            @pl.when(place == 3)
            def _():
                xm_copy(s, u).start()

    def turn_step(u):
        xm_copy(0, u).wait_recv()
        xm_copy(1, u).wait_recv()
        value, slope = gelu_pair(part[u, 0].astype(F32) + from_mid[u, 0].astype(F32))
        H[held_at(u, 1)] = ((part[u, 1].astype(F32) + from_mid[u, 1].astype(F32)) * slope).astype(BF16)
        ag_copy(1, u).start()
        H[held_at(u, 0)] = value.astype(BF16)
        ag_copy(0, u).start()
        spread(u)

    def pass_on(u):
        for s in (1, 0):
            ag_copy(s, u).wait_recv()

            @pl.when(place > 0)
            def _():
                ag_copy(s, u).start()

            if s:
                spread(u)

    up_x = []
    attn_block = attn_all.at[attn_rows(gz), :]
    own_up, own_proj = up_all.at[gz], proj_all.at[gz]
    for u in range(2 * steps):
        if u < steps:
            k, kind = units_order[u]
            if k == 0 and kind:
                arrive(own_c)
            if k and kind == 0:
                acquire(k - 1)
                if k == 2:
                    up_x += [put(own_up, own_up, xpeer(d)) for d in near_first]
            products(u)
            reduce_step(u)
        if u == 11:
            up_c = [put(own_up, own_up, core)]
            hand_over(up_x, lambda block: up_all.at[block], up_c)
        for where, lag in enumerate(lags):
            if lag <= u < lag + steps:
                @pl.when(place == where)
                def _():
                    (turn_step if where == 3 else pass_on)(u - lag)

    proj_x = [put(own_proj, own_proj, xpeer(d)) for d in near_first]
    proj_c = [put(own_proj, own_proj, core)]
    for copy in attn_z:
        arrive(copy)
    attn_x = [put(attn_block, attn_block, xpeer(d)) for d in near_first]
    attn_c = [put(attn_block, attn_block, core)]

    def drain_spread(act):
        for k in range(4):
            for kind in range(2):
                if k or kind:
                    act(dp_copy(k, kind))

    for copy in up_c:
        arrive(copy)
    for u, (k, kind) in enumerate(units_order):
        if u:
            dp_copy(k, kind).wait_recv()
        source = lax.rem(x + (0, 2, 1, 3)[k], 4) * 2 + half_of(kind)
        product = dot(HG[source], up_all[source], (0, 0))
        back[...] = back[...] + product if u else product
    total_t = back[...].T
    back_send[...] = total_t.astype(BF16)
    y_rows_of = lambda d: pl.ds(pl.multiple_of(lax.rem(y + d, 4) * 2 * feats, 32), 2 * feats)
    y_sum = [put(back_send.at[y_rows_of(d), :], yr.at[d - 1], ypeer(d)) for d in (1, 3, 2)]

    def joined(ref, t, s):
        return jnp.concatenate([ref[t, 0, s], ref[t, 1, s]], 1)

    def grad_weight(s, g, out):
        acc[...] = dot(joined(H, 0, s), joined(G, 0, g), (1, 1))

        def step(t, carry):
            acc[...] += dot(joined(H, t, s), joined(G, t, g), (1, 1))
            return carry

        lax.fori_loop(1, 4, step, 0)
        out[...] = (acc[...] * factor).astype(BF16)

    grad_weight(1, 0, gup_ref)
    for copy in y_sum:
        arrive(copy)
    total = back_send[y_rows, :].astype(F32)
    for d in range(3):
        total = total + yr[d].astype(F32)
    tot[...] = total
    tot[h_rows, :] += og[...].astype(F32)
    t_send[...] = tot[...].astype(BF16)
    h_sum = put(t_send, hr, hpeer)
    hand_over(proj_x, lambda block: proj_all.at[block], proj_c)
    grad_weight(0, 1, gdown_ref)
    arrive(gate_copy)
    arrive(h_sum)
    total = tot[...] + hr[...].astype(F32)
    GM[y_rows, :] = (total * gates[...].astype(F32)).astype(BF16)
    gm_y = [put(GM.at[y_rows, :], GM.at[y_rows, :], ypeer(d)) for d in (1, 3, 2)]
    tot[...] = total
    gmid_ref[...] = tot[h_rows, :].astype(BF16)
    for copy in proj_c:
        arrive(copy)

    def feat_rows(g):
        return pl.ds(pl.multiple_of(g * feats, 16), feats)

    def proj_part(pair):
        return sum(dot(GM[feat_rows(pair * 2 + n), :], proj_all[pair * 2 + n], (0, 0)) for n in range(2))

    back[...] = proj_part(y)
    for copy, d in zip(gm_y, (1, 3, 2)):
        arrive(copy)
        back[...] += proj_part(lax.rem(y - d + 4, 4))

    ap[...] = back[...].astype(BF16).reshape(ap.shape)
    ar_copies = [put(ap.at[lax.rem(a + d, 8)], ar.at[d - 1], gxpeer(d)) for d in (4, 3, 5, 2, 6, 1, 7)]
    gp_copies = []
    for d in range(1, 8):
        gp_copies.append(put(GM.at[feat_rows(lax.rem(gz + d, 8)), :], GP.at[gz], gzpeer(d)))
    GP[gz] = GM[feat_rows(gz), :]
    hand_over(attn_x, lambda block: attn_all.at[attn_rows(block), :], attn_c)
    for copy in attn_c:
        arrive(copy)
    for copy in gp_copies:
        arrive(copy)
    gproj_ref[...] = (dot(jnp.concatenate([GP[g] for g in range(8)], 1), attn_all[...], (1, 0)) * factor).astype(BF16)
    for copy in ar_copies:
        arrive(copy)
    total = ap[a].astype(F32)
    for d in range(7):
        total = total + ar[d].astype(F32)
    gattn_ref[...] = total.astype(BF16)

    finish(True)


def write_out(*refs):
    sources, targets, sems = refs[:5], refs[5:10], refs[10]
    copies = [
        pltpu.make_async_copy(source, target, sems.at[n])
        for n, (source, target) in enumerate(zip(sources, targets))
    ]
    for copy in copies:
        copy.start()
    for copy in copies:
        copy.wait()


def per_device(
    mid_stream, out_grad, attn_values, attn_gate, ffn_gate, up_weight, down_weight, proj_weight
):
    toks, feats = mid_stream.shape
    units, wide = up_weight.shape
    tok_total = toks * lax.axis_size("gz")
    factor = float(tok_total) ** (-0.5)
    vmem = pl.BlockSpec(memory_space=pltpu.VMEM)
    anywhere = pl.BlockSpec(memory_space=pl.ANY)
    dma = pltpu.SemaphoreType.DMA
    scratch = [
        pltpu.VMEM((4, 2, 2, wide, toks), BF16),
        pltpu.VMEM((2, 2, units, toks), F32),
        pltpu.VMEM((8, 2, units, toks), BF16),
        pltpu.VMEM((8, 2, units, toks), BF16),
        pltpu.VMEM((8, 2, units, toks), BF16),
        pltpu.VMEM((4, 2, 2, units, toks), BF16),
        pltpu.VMEM((8, units, wide), BF16),
        pltpu.VMEM((units, wide), BF16),
        pltpu.VMEM((8, feats, wide), BF16),
        pltpu.VMEM((tok_total, wide), BF16),
        pltpu.VMEM((2 * feats, toks), BF16),
        pltpu.VMEM((feats, toks), BF16),
        pltpu.VMEM((1, feats), BF16),
        pltpu.VMEM((1, feats), BF16),
        pltpu.VMEM((8, units, toks), BF16),
        pltpu.VMEM((toks, wide), F32),
        pltpu.VMEM((2 * feats, toks), F32),
        pltpu.VMEM((wide, toks), BF16),
        pltpu.VMEM((3, 2 * feats, toks), BF16),
        pltpu.VMEM((2 * feats, toks), BF16),
        pltpu.VMEM((2 * feats, toks), BF16),
        pltpu.VMEM((wide, toks), BF16),
        pltpu.VMEM((8, feats, toks), BF16),
        pltpu.VMEM((8, toks // 8, wide), BF16),
        pltpu.VMEM((7, toks // 8, wide), BF16),
        pltpu.VMEM((units, wide), F32),
        *[dma((8, 2))] * 6,
        dma((4, 2)), dma((4, 2)), dma((96,)), dma((96,)), dma((8,)),
    ]
    shape = jax.ShapeDtypeStruct
    shapes = (
        shape((feats, toks), BF16),
        shape((attn_values.shape[0], wide), BF16),
        shape((feats, wide), BF16),
        shape((units, wide), BF16),
        shape((units, wide), BF16),
    )
    results = pl.pallas_call(
        functools.partial(kernel, factor),
        out_shape=shapes,
        in_specs=[pl.BlockSpec(memory_space=pltpu.HBM)] * 8,
        out_specs=(vmem,) * 5,
        scratch_shapes=scratch,
        compiler_params=pltpu.CompilerParams(
            collective_id=0, has_side_effects=True, vmem_limit_bytes=63 * 1024 * 1024
        ),
        cost_estimate=pl.CostEstimate(flops=2_500_000_000, bytes_accessed=3_000_000, transcendentals=0),
        name="block_backward",
    )(
        mid_stream.T, out_grad.T, attn_values, attn_gate.reshape(1, feats), ffn_gate.reshape(1, feats),
        up_weight, down_weight, proj_weight,
    )
    grad_mid, *others = pl.pallas_call(
        write_out,
        out_shape=shapes,
        in_specs=[vmem] * 5,
        out_specs=(anywhere,) * 5,
        scratch_shapes=[dma((5,))],
        cost_estimate=pl.CostEstimate(flops=0, bytes_accessed=3_000_000, transcendentals=0),
        name="write_out",
    )(*results)
    return (grad_mid.T, *others)


def solution(mesh):
    return jax.shard_map(
        per_device,
        mesh=mesh,
        in_specs=(
            P("gz", ("gx", "gy")),
            P("gz", ("gx", "gy")),
            P(("gz", "gx"), "gy"),
            P(("gx", "gy")),
            P(("gx", "gy")),
            P(("gy", "gz"), "gx"),
            P(("gy", "gz"), "gx"),
            P(("gx", "gz"), "gy"),
        ),
        out_specs=(
            P("gz", ("gx", "gy")),
            P(("gz", "gx"), "gy"),
            P(("gx", "gz"), "gy"),
            P(("gy", "gz"), "gx"),
            P(("gy", "gz"), "gx"),
        ),
        check_vma=False,
    )
```

```python
import functools

import jax
import jax.numpy as jnp
from jax import lax
from jax.experimental import pallas as pl
from jax.experimental.pallas import tpu as pltpu
from jax.sharding import PartitionSpec as P

MESH = pl.DeviceIdType.MESH
BF16, F32 = jnp.bfloat16, jnp.float32
root_two_pi = 0.7978845608028654
cubic_term = 0.044715


def dot(former, latter, contract):
    return lax.dot_general(
        former, latter, ((contract[:1], contract[1:]), ((), ())), preferred_element_type=F32
    )


def gelu_pair(values):
    square = values * values
    tangent = jnp.tanh(root_two_pi * (values + cubic_term * values * square))
    half = 0.5 * (1.0 + tangent)
    slope = half + 0.5 * values * (1.0 - tangent * tangent) * root_two_pi * (
        1.0 + 3.0 * cubic_term * square
    )
    return values * half, slope


def kernel(
    factor,
    mid_in, out_in, attn_in, agate_in, fgate_in, up_in, down_in, proj_in,
    gmid_ref, gattn_ref, gproj_ref, gup_ref, gdown_ref,
    G, term, part, from_outer, from_mid, H, up_all, down_own, proj_all, attn_all, gates, og, ag_row, fg_row,
    HG, back, tot, back_send, yr, t_send, hr, GM, GP, ap, ar, acc,
    rs_s, rs_r, xm_s, xm_r, ag_s, ag_r, dp_s, dp_r, send_sems, recv_sems, local_sems,
):
    feats, toks = mid_in.shape
    units = up_in.shape[0]
    units_order = ((0, 0), (1, 0), (1, 1), (2, 0), (2, 1), (3, 0), (3, 1), (0, 1))
    steps = len(units_order)
    lags = (steps, 6, 4, 1)
    a = lax.axis_index("gx")
    gy = lax.axis_index("gy")
    gz = lax.axis_index("gz")
    x, c = gz // 2, lax.rem(gz, 2)
    y, h = gy // 2, lax.rem(gy, 2)

    def xpeer(d):
        return {"gz": lax.rem(x + d, 4) * 2 + c}

    def ypeer(d):
        return {"gy": lax.rem(y + d, 4) * 2 + h}

    core = {"gz": x * 2 + 1 - c}
    hpeer = {"gy": y * 2 + 1 - h}

    def gxpeer(d):
        return {"gx": lax.rem(a + d, 8)}

    def gzpeer(d):
        return {"gz": lax.rem(gz + d, 8)}

    barrier = pltpu.get_barrier_semaphore()
    peers = [gzpeer(d) for d in range(1, 8)] + [gxpeer(d) for d in range(1, 8)]
    peers += [ypeer(d) for d in range(1, 4)] + [hpeer]
    for peer in peers:
        pl.semaphore_signal(barrier, inc=1, device_id=peer, device_id_type=MESH)

    sent, open_recv = [], []
    count = [0]

    def put(src, dst, peer):
        index = count[0]
        count[0] += 1
        copy = pltpu.make_async_remote_copy(
            src, dst, send_sems.at[index], recv_sems.at[index],
            device_id=peer, device_id_type=MESH,
        )
        copy.start()
        sent.append(copy)
        open_recv.append(copy)
        return copy

    def arrive(copy):
        copy.wait_recv()
        open_recv[:] = [other for other in open_recv if other is not copy]

    def finish(line):
        for copy in open_recv:
            copy.wait_recv()
        for copy in sent:
            copy.wait_send()
        if not line:
            return

        for u in range(steps):
            for s in range(2):
                for r in range(pieces):
                    @pl.when(place < 3)
                    def _():
                        rs_copy(s, u, r).wait_send()

                    @pl.when(place == 3)
                    def _():
                        xm_copy(s, u, r).wait_send()

                    @pl.when(place > 0)
                    def _():
                        ag_copy(s, u, r).wait_send()

        drain_spread(lambda copy: copy.wait_send())

    own_rows = pl.ds(pl.multiple_of(gy * feats, 16), feats)
    y_rows = pl.ds(pl.multiple_of(y * 2 * feats, 32), 2 * feats)
    h_rows = pl.ds(pl.multiple_of(h * feats, 16), feats)

    partner_rows = pl.ds(pl.multiple_of((y * 2 + 1 - h) * feats, 16), feats)
    attn_row = pl.ds(pl.multiple_of((gz * 8 + a) * 16, 16), 16)

    loads = [
        pltpu.make_async_copy(src, dst, local_sems.at[n])
        for n, (src, dst) in enumerate((
            (mid_in, G.at[x, c, 0, own_rows, :]),
            (out_in, og),
            (fgate_in, fg_row),
            (agate_in, ag_row),
            (up_in, up_all.at[gz]),
            (down_in, down_own),
            (proj_in, proj_all.at[gz]),
            (attn_in, attn_all.at[attn_row, :]),
        ))
    ]
    for load in loads:
        load.start()
    for load in loads[:4]:
        load.wait()

    def gate_columns(row):
        return jnp.broadcast_to(row[...].astype(F32), (toks, feats)).T

    G[x, c, 1, own_rows, :] = (og[...].astype(F32) * gate_columns(fg_row)).astype(BF16)
    gates[h_rows, :] = gate_columns(ag_row).astype(BF16)
    for load in loads[4:]:
        load.wait()

    pl.semaphore_wait(barrier, len(peers))

    near_first = (2, 1, 3)

    def block_from(d):
        return lax.rem(x - d + 4, 4)

    h_copy = put(G.at[x, c, :, own_rows, :], G.at[x, c, :, own_rows, :], hpeer)
    own_y = [put(G.at[x, c, :, own_rows, :], G.at[x, c, :, own_rows, :], ypeer(d)) for d in near_first]
    gat_x = [[put(G.at[x, c, 1, own_rows, :], G.at[x, c, 1, own_rows, :], xpeer(d))] for d in near_first]
    arrive(h_copy)
    own_y += [
        put(G.at[x, c, :, partner_rows, :], G.at[x, c, :, partner_rows, :], ypeer(d)) for d in near_first
    ]
    for copies, d in zip(gat_x, near_first):
        copies.append(put(G.at[x, c, 1, partner_rows, :], G.at[x, c, 1, partner_rows, :], xpeer(d)))
    own_attn = attn_all.at[attn_row, :]
    attn_z = [put(own_attn, own_attn, gxpeer(d)) for d in range(1, 8)]
    gate_copy = put(gates.at[h_rows, :], gates.at[h_rows, :], hpeer)
    for copy in own_y:
        arrive(copy)
    own_c = put(G.at[x, c], G.at[x, c], core)
    mid_x = [put(G.at[x, c, 0], G.at[x, c, 0], xpeer(d)) for d in near_first]
    gat_y = []
    for copies, d in zip(gat_x, near_first):
        for copy in copies:
            arrive(copy)
        rows = G.at[block_from(d), c, 1, y_rows, :]
        gat_y.append([put(rows, rows, ypeer(e)) for e in near_first])

    def acquire(n):
        block = block_from(near_first[n])
        arrive(mid_x[n])
        mid_rows, gat_rows = G.at[block, c, 0], G.at[block, c, 1]
        halves = [put(mid_rows, mid_rows, core)]
        for copy in gat_y[n]:
            arrive(copy)
        halves.append(put(gat_rows, gat_rows, core))
        for copy in halves:
            arrive(copy)

    def attn_rows(block):
        return pl.ds(pl.multiple_of(block * toks, toks), toks)

    def hand_over(copies, ref_of, held):
        for copy, d in zip(copies, near_first):
            arrive(copy)
            block = block_from(d) * 2 + c
            held.append(put(ref_of(block), ref_of(block), core))

    near = a < 4
    place = jnp.where(near, a, 7 - a)
    inner = {"gx": jnp.where(near, a + 1, a - 1)}
    outer = {"gx": jnp.clip(jnp.where(near, a - 1, a + 1), 0, 7)}
    def block_of(k):
        return lax.rem(x + (0, 2, 3, 1)[k], 4)

    def rs_copy(s, u, r):
        return pltpu.make_async_remote_copy(
            part.at[u, s, rows_of(r)], from_outer.at[u, s, rows_of(r)], rs_s.at[u, s, r], rs_r.at[u, s, r],
            device_id=inner, device_id_type=MESH)

    def xm_copy(s, u, r):
        return pltpu.make_async_remote_copy(
            part.at[u, s, rows_of(r)], from_mid.at[u, s, rows_of(r)], xm_s.at[u, s, r], xm_r.at[u, s, r],
            device_id=inner, device_id_type=MESH)

    pieces = rs_s.shape[2]

    def rows_of(r):
        return pl.ds(r * (units // pieces), units // pieces)

    def held_at(u, s):
        k, kind = units_order[u]
        return block_of(k), half_of(kind), s

    def half_of(kind):
        return 1 - c if kind else c

    def ag_copy(s, u, r):
        t, half, _ = held_at(u, s)
        rows = H.at[t, half, s, rows_of(r)]
        return pltpu.make_async_remote_copy(
            rows, rows, ag_s.at[u, s, r], ag_r.at[u, s, r],
            device_id=outer, device_id_type=MESH)

    def dp_copy(k, kind):
        t, half = block_of(k), half_of(kind)
        return pltpu.make_async_remote_copy(
            H.at[t, half, 1], HG.at[gz], dp_s.at[k, kind], dp_r.at[k, kind],
            device_id={"gz": t * 2 + half}, device_id_type=MESH)

    def spread(u):
        k, kind = units_order[u]
        if k or kind:
            dp_copy(k, kind).start()
        else:
            HG[gz] = H[x, c, 1]

    def products(u):
        t, half, _ = held_at(u, 0)
        term[u % 2, 0] = dot(up_all[gz], G[t, half, 0], (1, 0))
        term[u % 2, 1] = dot(down_own[...], G[t, half, 1], (1, 0))

    def reduce_step(u):
        kind = u % 2
        for r in range(pieces):
            rows = rows_of(r)
            for s in range(2):
                @pl.when(place == 0)
                def _():
                    part[u, s, rows] = term[kind, s, rows].astype(BF16)

                @pl.when(place > 0)
                def _():
                    rs_copy(s, u, r).wait_recv()
                    part[u, s, rows] = (term[kind, s, rows] + from_outer[u, s, rows].astype(F32)).astype(BF16)

                @pl.when(place < 3)
                def _():
                    rs_copy(s, u, r).start()

                @pl.when(place == 3)
                def _():
                    xm_copy(s, u, r).start()

    def turn_step(u):
        t, half, _ = held_at(u, 0)
        for r in range(pieces):
            rows = rows_of(r)
            xm_copy(0, u, r).wait_recv()
            xm_copy(1, u, r).wait_recv()
            value, slope = gelu_pair(part[u, 0, rows].astype(F32) + from_mid[u, 0, rows].astype(F32))
            grad = part[u, 1, rows].astype(F32) + from_mid[u, 1, rows].astype(F32)
            H[t, half, 1, rows] = (grad * slope).astype(BF16)
            ag_copy(1, u, r).start()
            H[t, half, 0, rows] = value.astype(BF16)
        for r in range(pieces):
            ag_copy(0, u, r).start()
        spread(u)

    def pass_on(u):
        for s in (1, 0):
            for r in range(pieces):
                ag_copy(s, u, r).wait_recv()

                @pl.when(place > 0)
                def _():
                    ag_copy(s, u, r).start()

            if s:
                spread(u)

    up_x = []
    attn_block = attn_all.at[attn_rows(gz), :]
    own_up, own_proj = up_all.at[gz], proj_all.at[gz]
    for u in range(2 * steps):
        if u < steps:
            k, kind = units_order[u]
            if k == 0 and kind:
                arrive(own_c)
            if k and kind == 0:
                acquire(k - 1)
                if k == 1:
                    up_x += [put(own_up, own_up, xpeer(d)) for d in near_first]
            products(u)
            reduce_step(u)
        if u == 11:
            up_c = [put(own_up, own_up, core)]
            hand_over(up_x, lambda block: up_all.at[block], up_c)
        for where, lag in enumerate(lags):
            if lag <= u < lag + steps:
                @pl.when(place == where)
                def _():
                    (turn_step if where == 3 else pass_on)(u - lag)

    proj_x = [put(own_proj, own_proj, xpeer(d)) for d in near_first]
    proj_c = [put(own_proj, own_proj, core)]
    for copy in attn_z:
        arrive(copy)
    attn_x = [put(attn_block, attn_block, xpeer(d)) for d in near_first]
    attn_c = [put(attn_block, attn_block, core)]

    def drain_spread(act):
        for k in range(4):
            for kind in range(2):
                if k or kind:
                    act(dp_copy(k, kind))

    for copy in up_c:
        arrive(copy)
    for u, (k, kind) in enumerate(units_order):
        if u:
            dp_copy(k, kind).wait_recv()
        source = lax.rem(x + (0, 2, 1, 3)[k], 4) * 2 + half_of(kind)
        product = dot(HG[source], up_all[source], (0, 0))
        back[...] = back[...] + product if u else product
    total_t = back[...].T
    back_send[...] = total_t.astype(BF16)
    def feat_rows(g):
        return pl.ds(pl.multiple_of(g * feats, 16), feats)

    def y_block(d, n):
        return feat_rows(lax.rem(y + d, 4) * 2 + n)

    y_sum = [
        [put(back_send.at[y_block(d, n), :], yr.at[n, d - 1], ypeer(d)) for d in (1, 3, 2)] for n in range(2)
    ]

    def joined(ref, t, s):
        return jnp.concatenate([ref[t, 0, s], ref[t, 1, s]], 1)

    def grad_weight(s, g, out):
        acc[...] = dot(joined(H, 0, s), joined(G, 0, g), (1, 1))

        def step(t, carry):
            acc[...] += dot(joined(H, t, s), joined(G, t, g), (1, 1))
            return carry

        lax.fori_loop(1, 4, step, 0)
        out[...] = (acc[...] * factor).astype(BF16)

    h_sum, gm_y = [], []
    for n in range(2):
        for copy in y_sum[n]:
            arrive(copy)
        total = back_send[y_block(0, n), :].astype(F32) + jnp.where(h == n, 1.0, 0.0) * og[...].astype(F32)
        for d in range(3):
            total = total + yr[n, d].astype(F32)
        tot[n] = total
        t_send[n] = total.astype(BF16)
        h_sum.append(put(t_send.at[n], hr.at[n], hpeer))
    grad_weight(1, 0, gup_ref)
    hand_over(proj_x, lambda block: proj_all.at[block], proj_c)
    grad_weight(0, 1, gdown_ref)
    arrive(gate_copy)
    for n in range(2):
        arrive(h_sum[n])
        tot[n] += hr[n].astype(F32)
        block = y_block(0, n)
        GM[block, :] = (tot[n] * gates[pl.ds(n * feats, feats), :].astype(F32)).astype(BF16)
        gm_y.append([put(GM.at[block, :], GM.at[block, :], ypeer(d)) for d in (1, 3, 2)])
    gmid_ref[...] = tot[h].astype(BF16)
    for copy in proj_c:
        arrive(copy)

    def proj_part(g):
        return dot(GM[feat_rows(g), :], proj_all[g], (0, 0))

    back[...] = proj_part(y * 2) + proj_part(y * 2 + 1)
    for n in range(2):
        for copy, d in zip(gm_y[n], (1, 3, 2)):
            arrive(copy)
            back[...] += proj_part(lax.rem(y - d + 4, 4) * 2 + n)

    ap[...] = back[...].astype(BF16).reshape(ap.shape)
    ar_copies = [put(ap.at[lax.rem(a + d, 8)], ar.at[d - 1], gxpeer(d)) for d in (4, 3, 5, 2, 6, 1, 7)]
    gp_copies = []
    for d in range(1, 8):
        gp_copies.append(put(GM.at[feat_rows(lax.rem(gz + d, 8)), :], GP.at[gz], gzpeer(d)))
    GP[gz] = GM[feat_rows(gz), :]
    hand_over(attn_x, lambda block: attn_all.at[attn_rows(block), :], attn_c)
    for copy in attn_c:
        arrive(copy)
    for copy in gp_copies:
        arrive(copy)
    gproj_ref[...] = (dot(jnp.concatenate([GP[g] for g in range(8)], 1), attn_all[...], (1, 0)) * factor).astype(BF16)
    for copy in ar_copies:
        arrive(copy)
    total = ap[a].astype(F32)
    for d in range(7):
        total = total + ar[d].astype(F32)
    gattn_ref[...] = total.astype(BF16)

    finish(True)


def write_out(*refs):
    sources, targets, sems = refs[:5], refs[5:10], refs[10]
    copies = [
        pltpu.make_async_copy(source, target, sems.at[n])
        for n, (source, target) in enumerate(zip(sources, targets))
    ]
    for copy in copies:
        copy.start()
    for copy in copies:
        copy.wait()


def per_device(
    mid_stream, out_grad, attn_values, attn_gate, ffn_gate, up_weight, down_weight, proj_weight
):
    toks, feats = mid_stream.shape
    units, wide = up_weight.shape
    tok_total = toks * lax.axis_size("gz")
    factor = float(tok_total) ** (-0.5)
    vmem = pl.BlockSpec(memory_space=pltpu.VMEM)
    anywhere = pl.BlockSpec(memory_space=pl.ANY)
    dma = pltpu.SemaphoreType.DMA
    pieces = 2
    scratch = [
        pltpu.VMEM((4, 2, 2, wide, toks), BF16),
        pltpu.VMEM((2, 2, units, toks), F32),
        pltpu.VMEM((8, 2, units, toks), BF16),
        pltpu.VMEM((8, 2, units, toks), BF16),
        pltpu.VMEM((8, 2, units, toks), BF16),
        pltpu.VMEM((4, 2, 2, units, toks), BF16),
        pltpu.VMEM((8, units, wide), BF16),
        pltpu.VMEM((units, wide), BF16),
        pltpu.VMEM((8, feats, wide), BF16),
        pltpu.VMEM((tok_total, wide), BF16),
        pltpu.VMEM((2 * feats, toks), BF16),
        pltpu.VMEM((feats, toks), BF16),
        pltpu.VMEM((1, feats), BF16),
        pltpu.VMEM((1, feats), BF16),
        pltpu.VMEM((8, units, toks), BF16),
        pltpu.VMEM((toks, wide), F32),
        pltpu.VMEM((2, feats, toks), F32),
        pltpu.VMEM((wide, toks), BF16),
        pltpu.VMEM((2, 3, feats, toks), BF16),
        pltpu.VMEM((2, feats, toks), BF16),
        pltpu.VMEM((2, feats, toks), BF16),
        pltpu.VMEM((wide, toks), BF16),
        pltpu.VMEM((8, feats, toks), BF16),
        pltpu.VMEM((8, toks // 8, wide), BF16),
        pltpu.VMEM((7, toks // 8, wide), BF16),
        pltpu.VMEM((units, wide), F32),
        *[dma((8, 2, pieces))] * 6,
        dma((4, 2)), dma((4, 2)), dma((112,)), dma((112,)), dma((8,)),
    ]
    shape = jax.ShapeDtypeStruct
    shapes = (
        shape((feats, toks), BF16),
        shape((attn_values.shape[0], wide), BF16),
        shape((feats, wide), BF16),
        shape((units, wide), BF16),
        shape((units, wide), BF16),
    )
    results = pl.pallas_call(
        functools.partial(kernel, factor),
        out_shape=shapes,
        in_specs=[pl.BlockSpec(memory_space=pltpu.HBM)] * 8,
        out_specs=(vmem,) * 5,
        scratch_shapes=scratch,
        compiler_params=pltpu.CompilerParams(
            collective_id=0, has_side_effects=True, vmem_limit_bytes=63 * 1024 * 1024
        ),
        cost_estimate=pl.CostEstimate(flops=2_500_000_000, bytes_accessed=3_000_000, transcendentals=0),
        name="block_backward",
    )(
        mid_stream.T, out_grad.T, attn_values, attn_gate.reshape(1, feats), ffn_gate.reshape(1, feats),
        up_weight, down_weight, proj_weight,
    )
    grad_mid, *others = pl.pallas_call(
        write_out,
        out_shape=shapes,
        in_specs=[vmem] * 5,
        out_specs=(anywhere,) * 5,
        scratch_shapes=[dma((5,))],
        cost_estimate=pl.CostEstimate(flops=0, bytes_accessed=3_000_000, transcendentals=0),
        name="write_out",
    )(*results)
    return (grad_mid.T, *others)


def solution(mesh):
    return jax.shard_map(
        per_device,
        mesh=mesh,
        in_specs=(
            P("gz", ("gx", "gy")),
            P("gz", ("gx", "gy")),
            P(("gz", "gx"), "gy"),
            P(("gx", "gy")),
            P(("gx", "gy")),
            P(("gy", "gz"), "gx"),
            P(("gy", "gz"), "gx"),
            P(("gx", "gz"), "gy"),
        ),
        out_specs=(
            P("gz", ("gx", "gy")),
            P(("gz", "gx"), "gy"),
            P(("gx", "gz"), "gy"),
            P(("gy", "gz"), "gx"),
            P(("gy", "gz"), "gx"),
        ),
        check_vma=False,
    )
```

```python
import functools

import jax
import jax.numpy as jnp
from jax import lax
from jax.experimental import pallas as pl
from jax.experimental.pallas import tpu as pltpu
from jax.sharding import PartitionSpec as P

MESH = pl.DeviceIdType.MESH
BF16, F32 = jnp.bfloat16, jnp.float32
root_two_pi = 0.7978845608028654
cubic_term = 0.044715


def dot(former, latter, contract):
    return lax.dot_general(
        former, latter, ((contract[:1], contract[1:]), ((), ())), preferred_element_type=F32
    )


def gelu_pair(values):
    square = values * values
    tangent = jnp.tanh(root_two_pi * (values + cubic_term * values * square))
    half = 0.5 * (1.0 + tangent)
    slope = half + 0.5 * values * (1.0 - tangent * tangent) * root_two_pi * (
        1.0 + 3.0 * cubic_term * square
    )
    return values * half, slope


def kernel(
    factor,
    mid_in, out_in, attn_in, agate_in, fgate_in, up_in, down_in, proj_in,
    gmid_ref, gattn_ref, gproj_ref, gup_ref, gdown_ref,
    G, term, part, from_outer, from_mid, H, up_all, down_own, proj_all, attn_all, gates, og, ag_row, fg_row,
    HG, back, tot, back_send, yr, t_send, hr, GM, GP, ap, ar, acc,
    rs_s, rs_r, xm_s, xm_r, ag_s, ag_r, dp_s, dp_r, send_sems, recv_sems, local_sems,
):
    feats, toks = mid_in.shape
    units = up_in.shape[0]
    units_order = ((0, 0), (1, 0), (1, 1), (2, 0), (2, 1), (3, 0), (3, 1), (0, 1))
    steps = len(units_order)
    lags = (steps, 6, 4, 1)
    a = lax.axis_index("gx")
    gy = lax.axis_index("gy")
    gz = lax.axis_index("gz")
    x, c = gz // 2, lax.rem(gz, 2)
    y, h = gy // 2, lax.rem(gy, 2)

    def xpeer(d):
        return {"gz": lax.rem(x + d, 4) * 2 + c}

    def ypeer(d):
        return {"gy": lax.rem(y + d, 4) * 2 + h}

    core = {"gz": x * 2 + 1 - c}
    hpeer = {"gy": y * 2 + 1 - h}

    def gxpeer(d):
        return {"gx": lax.rem(a + d, 8)}

    def gzpeer(d):
        return {"gz": lax.rem(gz + d, 8)}

    barrier = pltpu.get_barrier_semaphore()
    peers = [gzpeer(d) for d in range(1, 8)] + [gxpeer(d) for d in range(1, 8)]
    peers += [ypeer(d) for d in range(1, 4)] + [hpeer]
    for peer in peers:
        pl.semaphore_signal(barrier, inc=1, device_id=peer, device_id_type=MESH)

    sent, open_recv = [], []
    count = [0]

    def put(src, dst, peer):
        index = count[0]
        count[0] += 1
        copy = pltpu.make_async_remote_copy(
            src, dst, send_sems.at[index], recv_sems.at[index],
            device_id=peer, device_id_type=MESH,
        )
        copy.start()
        sent.append(copy)
        open_recv.append(copy)
        return copy

    def arrive(copy):
        copy.wait_recv()
        open_recv[:] = [other for other in open_recv if other is not copy]

    def finish(line):
        for copy in open_recv:
            copy.wait_recv()
        for copy in sent:
            copy.wait_send()
        if not line:
            return

        for u in range(steps):
            for s in range(2):
                for r in range(pieces):
                    @pl.when(place < 3)
                    def _():
                        rs_copy(s, u, r).wait_send()

                    @pl.when(place == 3)
                    def _():
                        xm_copy(s, u, r).wait_send()

                    @pl.when(place > 0)
                    def _():
                        ag_copy(s, u, r).wait_send()

        drain_spread(lambda copy: copy.wait_send())

    own_rows = pl.ds(pl.multiple_of(gy * feats, 16), feats)
    y_rows = pl.ds(pl.multiple_of(y * 2 * feats, 32), 2 * feats)
    h_rows = pl.ds(pl.multiple_of(h * feats, 16), feats)

    partner_rows = pl.ds(pl.multiple_of((y * 2 + 1 - h) * feats, 16), feats)
    attn_row = pl.ds(pl.multiple_of((gz * 8 + a) * 16, 16), 16)

    loads = [
        pltpu.make_async_copy(src, dst, local_sems.at[n])
        for n, (src, dst) in enumerate((
            (mid_in, G.at[x, c, 0, own_rows, :]),
            (out_in, og),
            (fgate_in, fg_row),
            (agate_in, ag_row),
            (up_in, up_all.at[gz]),
            (down_in, down_own),
            (proj_in, proj_all.at[gz]),
            (attn_in, attn_all.at[attn_row, :]),
        ))
    ]
    for load in loads:
        load.start()
    for load in loads[:4]:
        load.wait()

    def gate_columns(row):
        return jnp.broadcast_to(row[...].astype(F32), (toks, feats)).T

    G[x, c, 1, own_rows, :] = (og[...].astype(F32) * gate_columns(fg_row)).astype(BF16)
    gates[h_rows, :] = gate_columns(ag_row).astype(BF16)
    for load in loads[4:]:
        load.wait()

    pl.semaphore_wait(barrier, len(peers))

    near_first = (2, 1, 3)

    def block_from(d):
        return lax.rem(x - d + 4, 4)

    h_copy = [put(G.at[x, c, s, own_rows, :], G.at[x, c, s, own_rows, :], hpeer) for s in (1, 0)]
    own_y = [put(G.at[x, c, :, own_rows, :], G.at[x, c, :, own_rows, :], ypeer(d)) for d in near_first]
    gat_x = [[put(G.at[x, c, 1, own_rows, :], G.at[x, c, 1, own_rows, :], xpeer(d))] for d in near_first]
    for copy, s in zip(h_copy, (1, 0)):
        arrive(copy)
        arrived = G.at[x, c, s, partner_rows, :]
        own_y += [put(arrived, arrived, ypeer(d)) for d in near_first]
        if s:
            for copies, d in zip(gat_x, near_first):
                copies.append(put(arrived, arrived, xpeer(d)))
    own_attn = attn_all.at[attn_row, :]
    attn_z = [put(own_attn, own_attn, gxpeer(d)) for d in range(1, 8)]
    gate_copy = put(gates.at[h_rows, :], gates.at[h_rows, :], hpeer)
    for copy in own_y:
        arrive(copy)
    own_c = put(G.at[x, c], G.at[x, c], core)
    mid_x = [put(G.at[x, c, 0], G.at[x, c, 0], xpeer(d)) for d in near_first]
    gat_y = []
    for copies, d in zip(gat_x, near_first):
        for copy in copies:
            arrive(copy)
        rows = G.at[block_from(d), c, 1, y_rows, :]
        gat_y.append([put(rows, rows, ypeer(e)) for e in near_first])

    def acquire(n):
        block = block_from(near_first[n])
        arrive(mid_x[n])
        mid_rows, gat_rows = G.at[block, c, 0], G.at[block, c, 1]
        halves = [put(mid_rows, mid_rows, core)]
        for copy in gat_y[n]:
            arrive(copy)
        halves.append(put(gat_rows, gat_rows, core))
        for copy in halves:
            arrive(copy)

    def attn_rows(block):
        return pl.ds(pl.multiple_of(block * toks, toks), toks)

    def hand_over(copies, ref_of, held):
        for copy, d in zip(copies, near_first):
            arrive(copy)
            block = block_from(d) * 2 + c
            held.append(put(ref_of(block), ref_of(block), core))

    near = a < 4
    place = jnp.where(near, a, 7 - a)
    inner = {"gx": jnp.where(near, a + 1, a - 1)}
    outer = {"gx": jnp.clip(jnp.where(near, a - 1, a + 1), 0, 7)}
    def block_of(k):
        return lax.rem(x + (0, 2, 3, 1)[k], 4)

    def rs_copy(s, u, r):
        return pltpu.make_async_remote_copy(
            part.at[u, s, rows_of(r)], from_outer.at[u, s, rows_of(r)], rs_s.at[u, s, r], rs_r.at[u, s, r],
            device_id=inner, device_id_type=MESH)

    def xm_copy(s, u, r):
        return pltpu.make_async_remote_copy(
            part.at[u, s, rows_of(r)], from_mid.at[u, s, rows_of(r)], xm_s.at[u, s, r], xm_r.at[u, s, r],
            device_id=inner, device_id_type=MESH)

    pieces = rs_s.shape[2]

    def rows_of(r):
        return pl.ds(r * (units // pieces), units // pieces)

    def held_at(u, s):
        k, kind = units_order[u]
        return block_of(k), half_of(kind), s

    def half_of(kind):
        return 1 - c if kind else c

    def ag_copy(s, u, r):
        t, half, _ = held_at(u, s)
        rows = H.at[t, half, s, rows_of(r)]
        return pltpu.make_async_remote_copy(
            rows, rows, ag_s.at[u, s, r], ag_r.at[u, s, r],
            device_id=outer, device_id_type=MESH)

    def dp_copy(k, kind):
        t, half = block_of(k), half_of(kind)
        return pltpu.make_async_remote_copy(
            H.at[t, half, 1], HG.at[gz], dp_s.at[k, kind], dp_r.at[k, kind],
            device_id={"gz": t * 2 + half}, device_id_type=MESH)

    def spread(u):
        k, kind = units_order[u]
        if k or kind:
            dp_copy(k, kind).start()
        else:
            HG[gz] = H[x, c, 1]

    def products(u):
        t, half, _ = held_at(u, 0)
        term[u % 2, 0] = dot(up_all[gz], G[t, half, 0], (1, 0))
        term[u % 2, 1] = dot(down_own[...], G[t, half, 1], (1, 0))

    def reduce_step(u):
        kind = u % 2
        for r in range(pieces):
            rows = rows_of(r)
            for s in range(2):
                @pl.when(place == 0)
                def _():
                    part[u, s, rows] = term[kind, s, rows].astype(BF16)

                @pl.when(place > 0)
                def _():
                    rs_copy(s, u, r).wait_recv()
                    part[u, s, rows] = (term[kind, s, rows] + from_outer[u, s, rows].astype(F32)).astype(BF16)

                @pl.when(place < 3)
                def _():
                    rs_copy(s, u, r).start()

                @pl.when(place == 3)
                def _():
                    xm_copy(s, u, r).start()

    def turn_step(u):
        t, half, _ = held_at(u, 0)
        for r in range(pieces):
            rows = rows_of(r)
            xm_copy(0, u, r).wait_recv()
            xm_copy(1, u, r).wait_recv()
            value, slope = gelu_pair(part[u, 0, rows].astype(F32) + from_mid[u, 0, rows].astype(F32))
            grad = part[u, 1, rows].astype(F32) + from_mid[u, 1, rows].astype(F32)
            H[t, half, 1, rows] = (grad * slope).astype(BF16)
            ag_copy(1, u, r).start()
            H[t, half, 0, rows] = value.astype(BF16)
        for r in range(pieces):
            ag_copy(0, u, r).start()
        spread(u)

    def pass_on(u):
        for s in (1, 0):
            for r in range(pieces):
                ag_copy(s, u, r).wait_recv()

                @pl.when(place > 0)
                def _():
                    ag_copy(s, u, r).start()

            if s:
                spread(u)

    up_x = []
    attn_block = attn_all.at[attn_rows(gz), :]
    own_up, own_proj = up_all.at[gz], proj_all.at[gz]
    for u in range(2 * steps):
        if u < steps:
            k, kind = units_order[u]
            if k == 0 and kind:
                arrive(own_c)
            if k and kind == 0:
                acquire(k - 1)
                if k == 1:
                    up_x += [put(own_up, own_up, xpeer(d)) for d in near_first]
            products(u)
            reduce_step(u)
        if u == 11:
            up_c = [put(own_up, own_up, core)]
            hand_over(up_x, lambda block: up_all.at[block], up_c)
        for where, lag in enumerate(lags):
            if lag <= u < lag + steps:
                @pl.when(place == where)
                def _():
                    (turn_step if where == 3 else pass_on)(u - lag)

    proj_x = [put(own_proj, own_proj, xpeer(d)) for d in near_first]
    proj_c = [put(own_proj, own_proj, core)]
    for copy in attn_z:
        arrive(copy)
    attn_x = [put(attn_block, attn_block, xpeer(d)) for d in near_first]
    attn_c = [put(attn_block, attn_block, core)]

    def drain_spread(act):
        for k in range(4):
            for kind in range(2):
                if k or kind:
                    act(dp_copy(k, kind))

    for copy in up_c:
        arrive(copy)
    for u, (k, kind) in enumerate(units_order):
        if u:
            dp_copy(k, kind).wait_recv()
        source = lax.rem(x + (0, 2, 1, 3)[k], 4) * 2 + half_of(kind)
        product = dot(HG[source], up_all[source], (0, 0))
        back[...] = back[...] + product if u else product
    total_t = back[...].T
    back_send[...] = total_t.astype(BF16)
    def feat_rows(g):
        return pl.ds(pl.multiple_of(g * feats, 16), feats)

    def y_block(d, n):
        return feat_rows(lax.rem(y + d, 4) * 2 + n)

    y_sum = [
        [put(back_send.at[y_block(d, n), :], yr.at[n, d - 1], ypeer(d)) for d in (1, 3, 2)] for n in range(2)
    ]

    def joined(ref, t, s):
        return jnp.concatenate([ref[t, 0, s], ref[t, 1, s]], 1)

    def grad_weight(s, g, out):
        acc[...] = dot(joined(H, 0, s), joined(G, 0, g), (1, 1))

        def step(t, carry):
            acc[...] += dot(joined(H, t, s), joined(G, t, g), (1, 1))
            return carry

        lax.fori_loop(1, 4, step, 0)
        out[...] = (acc[...] * factor).astype(BF16)

    h_sum, gm_y = [], []
    for n in range(2):
        for copy in y_sum[n]:
            arrive(copy)
        total = back_send[y_block(0, n), :].astype(F32) + jnp.where(h == n, 1.0, 0.0) * og[...].astype(F32)
        for d in range(3):
            total = total + yr[n, d].astype(F32)
        tot[n] = total
        t_send[n] = total.astype(BF16)
        h_sum.append(put(t_send.at[n], hr.at[n], hpeer))
    grad_weight(1, 0, gup_ref)
    hand_over(proj_x, lambda block: proj_all.at[block], proj_c)
    grad_weight(0, 1, gdown_ref)
    arrive(gate_copy)
    for n in range(2):
        arrive(h_sum[n])
        tot[n] += hr[n].astype(F32)
        block = y_block(0, n)
        GM[block, :] = (tot[n] * gates[pl.ds(n * feats, feats), :].astype(F32)).astype(BF16)
        gm_y.append([put(GM.at[block, :], GM.at[block, :], ypeer(d)) for d in (1, 3, 2)])
    gmid_ref[...] = tot[h].astype(BF16)
    for copy in proj_c:
        arrive(copy)

    def proj_part(g):
        return dot(GM[feat_rows(g), :], proj_all[g], (0, 0))

    back[...] = proj_part(y * 2) + proj_part(y * 2 + 1)
    for n in range(2):
        for copy, d in zip(gm_y[n], (1, 3, 2)):
            arrive(copy)
            back[...] += proj_part(lax.rem(y - d + 4, 4) * 2 + n)

    ap[...] = back[...].astype(BF16).reshape(ap.shape)
    ar_copies = [put(ap.at[lax.rem(a + d, 8)], ar.at[d - 1], gxpeer(d)) for d in (4, 3, 5, 2, 6, 1, 7)]
    gp_copies = []
    for d in range(1, 8):
        gp_copies.append(put(GM.at[feat_rows(lax.rem(gz + d, 8)), :], GP.at[gz], gzpeer(d)))
    GP[gz] = GM[feat_rows(gz), :]
    hand_over(attn_x, lambda block: attn_all.at[attn_rows(block), :], attn_c)
    for copy in attn_c:
        arrive(copy)
    for copy in gp_copies:
        arrive(copy)
    gproj_ref[...] = (dot(jnp.concatenate([GP[g] for g in range(8)], 1), attn_all[...], (1, 0)) * factor).astype(BF16)
    for copy in ar_copies:
        arrive(copy)
    total = ap[a].astype(F32)
    for d in range(7):
        total = total + ar[d].astype(F32)
    gattn_ref[...] = total.astype(BF16)

    finish(True)


def write_out(*refs):
    sources, targets, sems = refs[:5], refs[5:10], refs[10]
    copies = [
        pltpu.make_async_copy(source, target, sems.at[n])
        for n, (source, target) in enumerate(zip(sources, targets))
    ]
    for copy in copies:
        copy.start()
    for copy in copies:
        copy.wait()


def per_device(
    mid_stream, out_grad, attn_values, attn_gate, ffn_gate, up_weight, down_weight, proj_weight
):
    toks, feats = mid_stream.shape
    units, wide = up_weight.shape
    tok_total = toks * lax.axis_size("gz")
    factor = float(tok_total) ** (-0.5)
    vmem = pl.BlockSpec(memory_space=pltpu.VMEM)
    anywhere = pl.BlockSpec(memory_space=pl.ANY)
    dma = pltpu.SemaphoreType.DMA
    pieces = 2
    scratch = [
        pltpu.VMEM((4, 2, 2, wide, toks), BF16),
        pltpu.VMEM((2, 2, units, toks), F32),
        pltpu.VMEM((8, 2, units, toks), BF16),
        pltpu.VMEM((8, 2, units, toks), BF16),
        pltpu.VMEM((8, 2, units, toks), BF16),
        pltpu.VMEM((4, 2, 2, units, toks), BF16),
        pltpu.VMEM((8, units, wide), BF16),
        pltpu.VMEM((units, wide), BF16),
        pltpu.VMEM((8, feats, wide), BF16),
        pltpu.VMEM((tok_total, wide), BF16),
        pltpu.VMEM((2 * feats, toks), BF16),
        pltpu.VMEM((feats, toks), BF16),
        pltpu.VMEM((1, feats), BF16),
        pltpu.VMEM((1, feats), BF16),
        pltpu.VMEM((8, units, toks), BF16),
        pltpu.VMEM((toks, wide), F32),
        pltpu.VMEM((2, feats, toks), F32),
        pltpu.VMEM((wide, toks), BF16),
        pltpu.VMEM((2, 3, feats, toks), BF16),
        pltpu.VMEM((2, feats, toks), BF16),
        pltpu.VMEM((2, feats, toks), BF16),
        pltpu.VMEM((wide, toks), BF16),
        pltpu.VMEM((8, feats, toks), BF16),
        pltpu.VMEM((8, toks // 8, wide), BF16),
        pltpu.VMEM((7, toks // 8, wide), BF16),
        pltpu.VMEM((units, wide), F32),
        *[dma((8, 2, pieces))] * 6,
        dma((4, 2)), dma((4, 2)), dma((112,)), dma((112,)), dma((8,)),
    ]
    shape = jax.ShapeDtypeStruct
    shapes = (
        shape((feats, toks), BF16),
        shape((attn_values.shape[0], wide), BF16),
        shape((feats, wide), BF16),
        shape((units, wide), BF16),
        shape((units, wide), BF16),
    )
    results = pl.pallas_call(
        functools.partial(kernel, factor),
        out_shape=shapes,
        in_specs=[pl.BlockSpec(memory_space=pltpu.HBM)] * 8,
        out_specs=(vmem,) * 5,
        scratch_shapes=scratch,
        compiler_params=pltpu.CompilerParams(
            collective_id=0, has_side_effects=True, vmem_limit_bytes=63 * 1024 * 1024
        ),
        cost_estimate=pl.CostEstimate(flops=2_500_000_000, bytes_accessed=3_000_000, transcendentals=0),
        name="block_backward",
    )(
        mid_stream.T, out_grad.T, attn_values, attn_gate.reshape(1, feats), ffn_gate.reshape(1, feats),
        up_weight, down_weight, proj_weight,
    )
    grad_mid, *others = pl.pallas_call(
        write_out,
        out_shape=shapes,
        in_specs=[vmem] * 5,
        out_specs=(anywhere,) * 5,
        scratch_shapes=[dma((5,))],
        cost_estimate=pl.CostEstimate(flops=0, bytes_accessed=3_000_000, transcendentals=0),
        name="write_out",
    )(*results)
    return (grad_mid.T, *others)


def solution(mesh):
    return jax.shard_map(
        per_device,
        mesh=mesh,
        in_specs=(
            P("gz", ("gx", "gy")),
            P("gz", ("gx", "gy")),
            P(("gz", "gx"), "gy"),
            P(("gx", "gy")),
            P(("gx", "gy")),
            P(("gy", "gz"), "gx"),
            P(("gy", "gz"), "gx"),
            P(("gx", "gz"), "gy"),
        ),
        out_specs=(
            P("gz", ("gx", "gy")),
            P(("gz", "gx"), "gy"),
            P(("gx", "gz"), "gy"),
            P(("gy", "gz"), "gx"),
            P(("gy", "gz"), "gx"),
        ),
        check_vma=False,
    )
```

```python
import functools

import jax
import jax.numpy as jnp
from jax import lax
from jax.experimental import pallas as pl
from jax.experimental.pallas import tpu as pltpu
from jax.sharding import PartitionSpec as P

MESH = pl.DeviceIdType.MESH
BF16, F32 = jnp.bfloat16, jnp.float32
root_two_pi = 0.7978845608028654
cubic_term = 0.044715


def dot(former, latter, contract):
    return lax.dot_general(
        former, latter, ((contract[:1], contract[1:]), ((), ())), preferred_element_type=F32
    )


def gelu_pair(values):
    square = values * values
    tangent = jnp.tanh(root_two_pi * (values + cubic_term * values * square))
    half = 0.5 * (1.0 + tangent)
    slope = half + 0.5 * values * (1.0 - tangent * tangent) * root_two_pi * (
        1.0 + 3.0 * cubic_term * square
    )
    return values * half, slope


def kernel(
    factor,
    mid_in, out_in, attn_in, agate_in, fgate_in, up_in, down_in, proj_in,
    gmid_ref, gattn_ref, gproj_ref, gup_ref, gdown_ref,
    G, term, part, from_outer, from_mid, H, up_all, down_own, proj_all, attn_all, gates, og, ag_row, fg_row,
    HG, back, tot, back_send, yr, t_send, hr, GM, GP, ap, ar, acc,
    rs_s, rs_r, xm_s, xm_r, ag_s, ag_r, dp_s, dp_r, send_sems, recv_sems, local_sems,
):
    feats, toks = mid_in.shape
    units = up_in.shape[0]
    units_order = ((0, 0), (1, 0), (1, 1), (2, 0), (2, 1), (3, 0), (3, 1), (0, 1))
    steps = len(units_order)
    lags = (steps, 6, 4, 1)
    a = lax.axis_index("gx")
    gy = lax.axis_index("gy")
    gz = lax.axis_index("gz")
    x, c = gz // 2, lax.rem(gz, 2)
    y, h = gy // 2, lax.rem(gy, 2)

    def xpeer(d):
        return {"gz": lax.rem(x + d, 4) * 2 + c}

    def ypeer(d):
        return {"gy": lax.rem(y + d, 4) * 2 + h}

    core = {"gz": x * 2 + 1 - c}
    hpeer = {"gy": y * 2 + 1 - h}

    def gxpeer(d):
        return {"gx": lax.rem(a + d, 8)}

    def gzpeer(d):
        return {"gz": lax.rem(gz + d, 8)}

    barrier = pltpu.get_barrier_semaphore()
    peers = [gzpeer(d) for d in range(1, 8)] + [gxpeer(d) for d in range(1, 8)]
    peers += [ypeer(d) for d in range(1, 4)] + [hpeer]
    for peer in peers:
        pl.semaphore_signal(barrier, inc=1, device_id=peer, device_id_type=MESH)

    sent, open_recv = [], []
    count = [0]

    def put(src, dst, peer):
        index = count[0]
        count[0] += 1
        copy = pltpu.make_async_remote_copy(
            src, dst, send_sems.at[index], recv_sems.at[index],
            device_id=peer, device_id_type=MESH,
        )
        copy.start()
        sent.append(copy)
        open_recv.append(copy)
        return copy

    def arrive(copy):
        copy.wait_recv()
        open_recv[:] = [other for other in open_recv if other is not copy]

    def settle_sent():
        for copy in sent:
            copy.wait_send()
        sent.clear()

    def settle_line():
        for u in range(steps):
            for s in range(2):
                for r in range(pieces):
                    @pl.when(place < 3)
                    def _():
                        rs_copy(s, u, r).wait_send()

                    @pl.when(place == 3)
                    def _():
                        xm_copy(s, u, r).wait_send()

                    @pl.when(place > 0)
                    def _():
                        ag_copy(s, u, r).wait_send()

        drain_spread(lambda copy: copy.wait_send())

    own_rows = pl.ds(pl.multiple_of(gy * feats, 16), feats)
    y_rows = pl.ds(pl.multiple_of(y * 2 * feats, 32), 2 * feats)
    h_rows = pl.ds(pl.multiple_of(h * feats, 16), feats)

    partner_rows = pl.ds(pl.multiple_of((y * 2 + 1 - h) * feats, 16), feats)
    attn_row = pl.ds(pl.multiple_of((gz * 8 + a) * 16, 16), 16)

    loads = [
        pltpu.make_async_copy(src, dst, local_sems.at[n])
        for n, (src, dst) in enumerate((
            (mid_in, G.at[x, c, 0, own_rows, :]),
            (out_in, og),
            (fgate_in, fg_row),
            (agate_in, ag_row),
            (up_in, up_all.at[gz]),
            (down_in, down_own),
            (proj_in, proj_all.at[gz]),
            (attn_in, attn_all.at[attn_row, :]),
        ))
    ]
    for load in loads:
        load.start()
    for load in loads[:4]:
        load.wait()

    def gate_columns(row):
        return jnp.broadcast_to(row[...].astype(F32), (toks, feats)).T

    G[x, c, 1, own_rows, :] = (og[...].astype(F32) * gate_columns(fg_row)).astype(BF16)

    pl.semaphore_wait(barrier, len(peers))

    near_first = (2, 1, 3)

    def block_from(d):
        return lax.rem(x - d + 4, 4)

    h_copy = [put(G.at[x, c, s, own_rows, :], G.at[x, c, s, own_rows, :], hpeer) for s in (1, 0)]
    own_y = [put(G.at[x, c, :, own_rows, :], G.at[x, c, :, own_rows, :], ypeer(d)) for d in near_first]
    gat_x = [[put(G.at[x, c, 1, own_rows, :], G.at[x, c, 1, own_rows, :], xpeer(d))] for d in near_first]
    gates[h_rows, :] = gate_columns(ag_row).astype(BF16)
    for load in loads[4:]:
        load.wait()
    for copy, s in zip(h_copy, (1, 0)):
        arrive(copy)
        arrived = G.at[x, c, s, partner_rows, :]
        own_y += [put(arrived, arrived, ypeer(d)) for d in near_first]
        if s:
            for copies, d in zip(gat_x, near_first):
                copies.append(put(arrived, arrived, xpeer(d)))
    own_attn = attn_all.at[attn_row, :]
    attn_z = [put(own_attn, own_attn, gxpeer(d)) for d in range(1, 8)]
    gate_copy = put(gates.at[h_rows, :], gates.at[h_rows, :], hpeer)
    for copy in own_y:
        arrive(copy)
    own_c = put(G.at[x, c], G.at[x, c], core)
    mid_x = [put(G.at[x, c, 0], G.at[x, c, 0], xpeer(d)) for d in near_first]
    gat_y = []
    for copies, d in zip(gat_x, near_first):
        for copy in copies:
            arrive(copy)
        rows = G.at[block_from(d), c, 1, y_rows, :]
        gat_y.append([put(rows, rows, ypeer(e)) for e in near_first])

    def acquire(n):
        block = block_from(near_first[n])
        arrive(mid_x[n])
        mid_rows, gat_rows = G.at[block, c, 0], G.at[block, c, 1]
        halves = [put(mid_rows, mid_rows, core)]
        for copy in gat_y[n]:
            arrive(copy)
        halves.append(put(gat_rows, gat_rows, core))
        for copy in halves:
            arrive(copy)

    def attn_rows(block):
        return pl.ds(pl.multiple_of(block * toks, toks), toks)

    def hand_over(copies, ref_of, held):
        for copy, d in zip(copies, near_first):
            arrive(copy)
            block = block_from(d) * 2 + c
            held.append(put(ref_of(block), ref_of(block), core))

    near = a < 4
    place = jnp.where(near, a, 7 - a)
    inner = {"gx": jnp.where(near, a + 1, a - 1)}
    outer = {"gx": jnp.clip(jnp.where(near, a - 1, a + 1), 0, 7)}
    def block_of(k):
        return lax.rem(x + (0, 2, 3, 1)[k], 4)

    def rs_copy(s, u, r):
        return pltpu.make_async_remote_copy(
            part.at[u, s, rows_of(r)], from_outer.at[u, s, rows_of(r)], rs_s.at[u, s, r], rs_r.at[u, s, r],
            device_id=inner, device_id_type=MESH)

    def xm_copy(s, u, r):
        return pltpu.make_async_remote_copy(
            part.at[u, s, rows_of(r)], from_mid.at[u, s, rows_of(r)], xm_s.at[u, s, r], xm_r.at[u, s, r],
            device_id=inner, device_id_type=MESH)

    pieces = rs_s.shape[2]

    def rows_of(r):
        return pl.ds(r * (units // pieces), units // pieces)

    def held_at(u, s):
        k, kind = units_order[u]
        return block_of(k), half_of(kind), s

    def half_of(kind):
        return 1 - c if kind else c

    def ag_copy(s, u, r):
        t, half, _ = held_at(u, s)
        rows = H.at[t, half, s, rows_of(r)]
        return pltpu.make_async_remote_copy(
            rows, rows, ag_s.at[u, s, r], ag_r.at[u, s, r],
            device_id=outer, device_id_type=MESH)

    def dp_copy(k, kind):
        t, half = block_of(k), half_of(kind)
        return pltpu.make_async_remote_copy(
            H.at[t, half, 1], HG.at[gz], dp_s.at[k, kind], dp_r.at[k, kind],
            device_id={"gz": t * 2 + half}, device_id_type=MESH)

    def spread(u):
        k, kind = units_order[u]
        if k or kind:
            dp_copy(k, kind).start()
        else:
            HG[gz] = H[x, c, 1]

    def products(u):
        t, half, _ = held_at(u, 0)
        term[u % 2, 0] = dot(up_all[gz], G[t, half, 0], (1, 0))
        term[u % 2, 1] = dot(down_own[...], G[t, half, 1], (1, 0))

    def reduce_step(u):
        kind = u % 2
        for r in range(pieces):
            rows = rows_of(r)
            for s in range(2):
                @pl.when(place == 0)
                def _():
                    part[u, s, rows] = term[kind, s, rows].astype(BF16)

                @pl.when(place > 0)
                def _():
                    rs_copy(s, u, r).wait_recv()
                    part[u, s, rows] = (term[kind, s, rows] + from_outer[u, s, rows].astype(F32)).astype(BF16)

                @pl.when(place < 3)
                def _():
                    rs_copy(s, u, r).start()

                @pl.when(place == 3)
                def _():
                    xm_copy(s, u, r).start()

    def turn_step(u):
        t, half, _ = held_at(u, 0)
        for r in range(pieces):
            rows = rows_of(r)
            xm_copy(0, u, r).wait_recv()
            xm_copy(1, u, r).wait_recv()
            value, slope = gelu_pair(part[u, 0, rows].astype(F32) + from_mid[u, 0, rows].astype(F32))
            grad = part[u, 1, rows].astype(F32) + from_mid[u, 1, rows].astype(F32)
            H[t, half, 1, rows] = (grad * slope).astype(BF16)
            ag_copy(1, u, r).start()
            H[t, half, 0, rows] = value.astype(BF16)
        for r in range(pieces):
            ag_copy(0, u, r).start()
        spread(u)

    def pass_on(u):
        for s in (1, 0):
            for r in range(pieces):
                ag_copy(s, u, r).wait_recv()

                @pl.when(place > 0)
                def _():
                    ag_copy(s, u, r).start()

            if s:
                spread(u)

    up_x = []
    attn_block = attn_all.at[attn_rows(gz), :]
    own_up, own_proj = up_all.at[gz], proj_all.at[gz]
    for u in range(2 * steps):
        if u < steps:
            k, kind = units_order[u]
            if k == 0 and kind:
                arrive(own_c)
            if k and kind == 0:
                acquire(k - 1)
                if k == 1:
                    up_x += [put(own_up, own_up, xpeer(d)) for d in near_first]
            products(u)
            reduce_step(u)
        if u == 11:
            up_c = [put(own_up, own_up, core)]
            hand_over(up_x, lambda block: up_all.at[block], up_c)
        for where, lag in enumerate(lags):
            if lag <= u < lag + steps:
                @pl.when(place == where)
                def _():
                    (turn_step if where == 3 else pass_on)(u - lag)

    proj_x = [put(own_proj, own_proj, xpeer(d)) for d in near_first]
    proj_c = [put(own_proj, own_proj, core)]
    for copy in attn_z:
        arrive(copy)
    attn_x = [put(attn_block, attn_block, xpeer(d)) for d in near_first]
    attn_c = [put(attn_block, attn_block, core)]

    def drain_spread(act):
        for k in range(4):
            for kind in range(2):
                if k or kind:
                    act(dp_copy(k, kind))

    for copy in up_c:
        arrive(copy)
    for u, (k, kind) in enumerate(units_order):
        if u:
            dp_copy(k, kind).wait_recv()
        source = lax.rem(x + (0, 2, 1, 3)[k], 4) * 2 + half_of(kind)
        product = dot(HG[source], up_all[source], (0, 0))
        back[...] = back[...] + product if u else product
    total_t = back[...].T
    back_send[...] = total_t.astype(BF16)
    def feat_rows(g):
        return pl.ds(pl.multiple_of(g * feats, 16), feats)

    def y_block(d, n):
        return feat_rows(lax.rem(y + d, 4) * 2 + n)

    y_sum = [
        [put(back_send.at[y_block(d, n), :], yr.at[n, d - 1], ypeer(d)) for d in (1, 3, 2)] for n in range(2)
    ]

    def joined(ref, t, s):
        return jnp.concatenate([ref[t, 0, s], ref[t, 1, s]], 1)

    def grad_weight(s, g, out):
        acc[...] = dot(joined(H, 0, s), joined(G, 0, g), (1, 1))

        def step(t, carry):
            acc[...] += dot(joined(H, t, s), joined(G, t, g), (1, 1))
            return carry

        lax.fori_loop(1, 4, step, 0)
        out[...] = (acc[...] * factor).astype(BF16)

    h_sum, gm_y = [], []
    for n in range(2):
        for copy in y_sum[n]:
            arrive(copy)
        total = back_send[y_block(0, n), :].astype(F32) + jnp.where(h == n, 1.0, 0.0) * og[...].astype(F32)
        for d in range(3):
            total = total + yr[n, d].astype(F32)
        tot[n] = total
        t_send[n] = total.astype(BF16)
        h_sum.append(put(t_send.at[n], hr.at[n], hpeer))
    grad_weight(1, 0, gup_ref)
    hand_over(proj_x, lambda block: proj_all.at[block], proj_c)
    grad_weight(0, 1, gdown_ref)
    arrive(gate_copy)
    for n in range(2):
        arrive(h_sum[n])
        tot[n] += hr[n].astype(F32)
        block = y_block(0, n)
        GM[block, :] = (tot[n] * gates[pl.ds(n * feats, feats), :].astype(F32)).astype(BF16)
        gm_y.append([put(GM.at[block, :], GM.at[block, :], ypeer(d)) for d in (1, 3, 2)])
    gmid_ref[...] = tot[h].astype(BF16)
    for copy in proj_c:
        arrive(copy)

    def proj_part(g):
        return dot(GM[feat_rows(g), :], proj_all[g], (0, 0))

    back[...] = proj_part(y * 2) + proj_part(y * 2 + 1)
    for n in range(2):
        for copy, d in zip(gm_y[n], (1, 3, 2)):
            arrive(copy)
            back[...] += proj_part(lax.rem(y - d + 4, 4) * 2 + n)

    earlier = list(sent)
    sent.clear()
    ap[...] = back[...].astype(BF16).reshape(ap.shape)
    ar_copies = [put(ap.at[lax.rem(a + d, 8)], ar.at[d - 1], gxpeer(d)) for d in (4, 3, 5, 2, 6, 1, 7)]
    gp_copies = []
    for d in range(1, 8):
        gp_copies.append(put(GM.at[feat_rows(lax.rem(gz + d, 8)), :], GP.at[gz], gzpeer(d)))
    GP[gz] = GM[feat_rows(gz), :]
    hand_over(attn_x, lambda block: attn_all.at[attn_rows(block), :], attn_c)
    settle_line()
    for copy in earlier:
        copy.wait_send()
    for copy in attn_c:
        arrive(copy)
    for copy in gp_copies:
        arrive(copy)
    gproj_ref[...] = (dot(jnp.concatenate([GP[g] for g in range(8)], 1), attn_all[...], (1, 0)) * factor).astype(BF16)
    for copy in ar_copies:
        arrive(copy)
    total = ap[a].astype(F32)
    for d in range(7):
        total = total + ar[d].astype(F32)
    gattn_ref[...] = total.astype(BF16)

    settle_sent()


def write_out(*refs):
    sources, targets, sems = refs[:5], refs[5:10], refs[10]
    copies = [
        pltpu.make_async_copy(source, target, sems.at[n])
        for n, (source, target) in enumerate(zip(sources, targets))
    ]
    for copy in copies:
        copy.start()
    for copy in copies:
        copy.wait()


def per_device(
    mid_stream, out_grad, attn_values, attn_gate, ffn_gate, up_weight, down_weight, proj_weight
):
    toks, feats = mid_stream.shape
    units, wide = up_weight.shape
    tok_total = toks * lax.axis_size("gz")
    factor = float(tok_total) ** (-0.5)
    vmem = pl.BlockSpec(memory_space=pltpu.VMEM)
    anywhere = pl.BlockSpec(memory_space=pl.ANY)
    dma = pltpu.SemaphoreType.DMA
    pieces = 2
    scratch = [
        pltpu.VMEM((4, 2, 2, wide, toks), BF16),
        pltpu.VMEM((2, 2, units, toks), F32),
        pltpu.VMEM((8, 2, units, toks), BF16),
        pltpu.VMEM((8, 2, units, toks), BF16),
        pltpu.VMEM((8, 2, units, toks), BF16),
        pltpu.VMEM((4, 2, 2, units, toks), BF16),
        pltpu.VMEM((8, units, wide), BF16),
        pltpu.VMEM((units, wide), BF16),
        pltpu.VMEM((8, feats, wide), BF16),
        pltpu.VMEM((tok_total, wide), BF16),
        pltpu.VMEM((2 * feats, toks), BF16),
        pltpu.VMEM((feats, toks), BF16),
        pltpu.VMEM((1, feats), BF16),
        pltpu.VMEM((1, feats), BF16),
        pltpu.VMEM((8, units, toks), BF16),
        pltpu.VMEM((toks, wide), F32),
        pltpu.VMEM((2, feats, toks), F32),
        pltpu.VMEM((wide, toks), BF16),
        pltpu.VMEM((2, 3, feats, toks), BF16),
        pltpu.VMEM((2, feats, toks), BF16),
        pltpu.VMEM((2, feats, toks), BF16),
        pltpu.VMEM((wide, toks), BF16),
        pltpu.VMEM((8, feats, toks), BF16),
        pltpu.VMEM((8, toks // 8, wide), BF16),
        pltpu.VMEM((7, toks // 8, wide), BF16),
        pltpu.VMEM((units, wide), F32),
        *[dma((8, 2, pieces))] * 6,
        dma((4, 2)), dma((4, 2)), dma((112,)), dma((112,)), dma((8,)),
    ]
    shape = jax.ShapeDtypeStruct
    shapes = (
        shape((feats, toks), BF16),
        shape((attn_values.shape[0], wide), BF16),
        shape((feats, wide), BF16),
        shape((units, wide), BF16),
        shape((units, wide), BF16),
    )
    results = pl.pallas_call(
        functools.partial(kernel, factor),
        out_shape=shapes,
        in_specs=[pl.BlockSpec(memory_space=pltpu.HBM)] * 8,
        out_specs=(vmem,) * 5,
        scratch_shapes=scratch,
        compiler_params=pltpu.CompilerParams(
            collective_id=0, has_side_effects=True, vmem_limit_bytes=63 * 1024 * 1024
        ),
        cost_estimate=pl.CostEstimate(flops=2_500_000_000, bytes_accessed=3_000_000, transcendentals=0),
        name="block_backward",
    )(
        mid_stream.T, out_grad.T, attn_values, attn_gate.reshape(1, feats), ffn_gate.reshape(1, feats),
        up_weight, down_weight, proj_weight,
    )
    grad_mid, *others = pl.pallas_call(
        write_out,
        out_shape=shapes,
        in_specs=[vmem] * 5,
        out_specs=(anywhere,) * 5,
        scratch_shapes=[dma((5,))],
        cost_estimate=pl.CostEstimate(flops=0, bytes_accessed=3_000_000, transcendentals=0),
        name="write_out",
    )(*results)
    return (grad_mid.T, *others)


def solution(mesh):
    return jax.shard_map(
        per_device,
        mesh=mesh,
        in_specs=(
            P("gz", ("gx", "gy")),
            P("gz", ("gx", "gy")),
            P(("gz", "gx"), "gy"),
            P(("gx", "gy")),
            P(("gx", "gy")),
            P(("gy", "gz"), "gx"),
            P(("gy", "gz"), "gx"),
            P(("gx", "gz"), "gy"),
        ),
        out_specs=(
            P("gz", ("gx", "gy")),
            P(("gz", "gx"), "gy"),
            P(("gx", "gz"), "gy"),
            P(("gy", "gz"), "gx"),
            P(("gy", "gz"), "gx"),
        ),
        check_vma=False,
    )
```
